128 devices in a mesh: loop: 16 (over y, z_lo, core), grp: 8 (over x, z_hi).
Axes of the slice: x: 4, y: 4, z: 4 (z_hi: 2, z_lo: 2; z = z_hi * 2 + z_lo), core: 2. Of those that a mesh axis runs over, the one named last changes fastest.
Arguments:
- patch_token_rows: bfloat16 [2048, 32, 1152], P(('loop', 'grp')), may hold values from -24 to 24
- probe_query_heads: float32 [1152], replicated, as said below
- key_value_matrix: bfloat16 [1152, 2304], replicated, may hold values from -0.1875 to 0.1875
- output_weight: bfloat16 [1152, 1152], replicated, may hold values from -0.1875 to 0.1875
- text_pooled_features: bfloat16 [2048, 1152], P(('loop', 'grp')), may hold values from -24 to 24
- text_head_weight: bfloat16 [1152, 1152], replicated, may hold values from -0.1875 to 0.1875
- log_logit_scale: float32 [1], replicated, may hold values from 4.2 to 4.8
- logit_bias_value: float32 [1], replicated, may hold values from -12 to -8
Outputs:
- grad_key_value: float32 [1152, 2304], P(('loop', 'grp'))
- grad_out: float32 [1152, 1152], P(('loop', 'grp'))
- grad_text: float32 [1152, 1152], P(('loop', 'grp'))
- grad_probe: float32 [1152], replicated
- text_feature_grad: bfloat16 [2048, 1152], P(('loop', 'grp'))
The draws below stay inside these ranges and needn't reach their ends.
Inputs may be any that keep to these rules, and one draw needn't show every extreme that they name: `probe_query_heads`: entries are finite reals of either sign.
All inputs are finite; a program needn't handle non-finite values.
Results may differ from the reference program's by a relative error of at most 0.017.
The reference program's roundings to bfloat16 on the way count: a program that leaves them out, or rounds other values in their place, can miss the bound.
Values may be sent and summed in bfloat16 or wider, within the bound.
A program may use at most 128 MiB of HBM per device.

```python
import math
import jax
import jax.numpy as jnp
from jax import lax

D = 1152
HEADS = 16
PATCH = 32
B_DEV = 16
IMAGES = 2048


def draw_probe_query_heads(key, part):
    key = jax.random.fold_in(key, 11)
    normal_key, spread_key = jax.random.split(key)
    normal_part = jax.random.normal(normal_key, (HEADS, D // HEADS), jnp.float32)
    spread = jax.random.uniform(spread_key, (HEADS, 1), jnp.float32, 0.5, 2.0)
    return (normal_part * spread).reshape(D)


def spiked(drawn, key, source, target, parts, factor):
    def block_of(dim):
        return (jnp.arange(drawn.shape[dim]) // (drawn.shape[dim] // parts)).reshape((-1,) + (1,) * (drawn.ndim - 1 - dim))

    first = jax.random.permutation(key, parts)[block_of(target)]
    other_side = (block_of(target) + parts // 2) % parts
    return jnp.where((block_of(source) == first) | (block_of(source) == other_side), factor * drawn, drawn)


def block_levels(rng, extent, shards, low, top_value):
    level = 1.0
    for dim, parts in shards:
        heights = jax.random.uniform(jax.random.fold_in(jax.random.fold_in(rng, 6), dim), (parts,), jnp.float32, low / len(shards), top_value / len(shards))
        level = level * jnp.repeat(jnp.exp(heights), extent[dim] // parts).reshape((-1,) + (1,) * (len(extent) - 1 - dim))
    return level


def normal_values(stream_key, dims, width, bound, shards=(), kind=jnp.bfloat16):
    drawn = width * jax.random.normal(stream_key, dims, jnp.float32)
    if shards:
        drawn = drawn * block_levels(stream_key, dims, shards, -0.22, 0.18)
    return jnp.clip(drawn, -bound, bound).astype(kind)


def bell_draw_with(stream_key, shape, scale, reach, shards, heavy, kind=jnp.bfloat16):
    array = scale * jax.random.normal(stream_key, shape, jnp.float32)
    if shards:
        array = array * block_levels(stream_key, shape, shards, -0.22, 0.18)
    return jnp.clip(spiked(array, jax.random.fold_in(stream_key, 3), *heavy), -reach, reach).astype(kind)


def setup_inputs(seed: int = 0) -> dict:
    key_list = jax.random.split(jax.random.key(seed), 9)
    patch_token_rows = bell_draw_with(key_list[0], (IMAGES, PATCH, D), 1.0, 24.0, ((0, 128),), (0, 2, 128, 5.5))
    probe_query_heads = draw_probe_query_heads(jax.random.fold_in(key_list[8], 71), 0)
    key_value_matrix = normal_values(key_list[2], (D, 2 * D), D ** -0.5, 0.1875)
    output_weight = normal_values(key_list[3], (D, D), D ** -0.5, 0.1875)
    text_pooled_features = bell_draw_with(key_list[4], (IMAGES, D), 1.0, 24.0, ((0, 128),), (0, 1, 128, 5.5))
    text_head_weight = normal_values(key_list[5], (D, D), D ** -0.5, 0.1875)
    log_logit_scale = jnp.clip(jax.random.uniform(key_list[6], (1,), jnp.float32, 4.2, 4.8), 4.2, 4.8)
    logit_bias_value = jnp.clip(jax.random.uniform(key_list[7], (1,), jnp.float32, -12.0, -8.0), -12.0, -8.0)
    return dict(patch_token_rows=patch_token_rows, probe_query_heads=probe_query_heads, key_value_matrix=key_value_matrix, output_weight=output_weight, text_pooled_features=text_pooled_features, text_head_weight=text_head_weight, log_logit_scale=log_logit_scale, logit_bias_value=logit_bias_value)


def unit_rows(values):
    lengths = jnp.sqrt(lax.optimization_barrier(jnp.sum(values * values, axis=1, keepdims=True)) + 1e-06)
    return (values / lengths, lengths)

def unit_backward(gradient, unit, lengths):
    return (gradient - unit * lax.optimization_barrier(jnp.sum(unit * gradient, axis=1, keepdims=True))) / lengths

def attend(image_batch, key_value_matrix, query_half, score_root):
    head_width = D // HEADS
    key_values = jnp.dot(image_batch.reshape(B_DEV * PATCH, D), key_value_matrix, preferred_element_type=jnp.float32).astype(jnp.bfloat16)
    key_values = key_values.reshape(B_DEV, PATCH, 2, HEADS, head_width)
    key_part = key_values[:, :, 0]
    value_part = key_values[:, :, 1]
    scores = jnp.einsum('nphe,he->nhp', key_part.astype(jnp.float32), query_half.astype(jnp.float32)) / score_root
    weights = jax.nn.softmax(scores, axis=-1)
    weights_half = weights.astype(jnp.bfloat16)
    return (key_part, value_part, weights, weights_half)

def reference(patch_token_rows, probe_query_heads, key_value_matrix, output_weight, text_pooled_features, text_head_weight, log_logit_scale, logit_bias_value):
    head_width = D // HEADS
    score_root = math.sqrt(head_width)
    logit_scale = jnp.exp(log_logit_scale[0])
    row_displacement = logit_bias_value[0]
    text_out = jnp.dot(text_pooled_features, text_head_weight, preferred_element_type=jnp.float32)
    text_unit, text_lengths = unit_rows(text_out)
    text_embedding = text_unit.astype(jnp.bfloat16)
    query_half = probe_query_heads.astype(jnp.bfloat16).reshape(HEADS, head_width)
    image_blocks = patch_token_rows.reshape(IMAGES // B_DEV, B_DEV, PATCH, D)

    def forward(image_batch):
        key_part, value_part, weights, weights_half = attend(image_batch, key_value_matrix, query_half, score_root)
        pooled = jnp.einsum('nhp,nphe->nhe', weights_half.astype(jnp.float32), value_part.astype(jnp.float32))
        return pooled.astype(jnp.bfloat16).reshape(B_DEV, D)
    pooled = lax.map(forward, image_blocks).reshape(IMAGES, D)
    image_out = jnp.dot(pooled, output_weight, preferred_element_type=jnp.float32)
    image_unit, image_lengths = unit_rows(image_out)
    image_embedding = image_unit.astype(jnp.bfloat16)
    similarity_scores = jnp.dot(image_embedding, text_embedding.T, preferred_element_type=jnp.float32)
    logit_matrix = logit_scale * similarity_scores + row_displacement
    row_ids = jnp.arange(IMAGES, dtype=jnp.int32)
    pair_sign = jnp.where(row_ids[:, None] == row_ids[None, :], 1.0, -1.0).astype(jnp.float32)
    pair_factor = (-pair_sign * jax.nn.sigmoid(-pair_sign * logit_matrix)).astype(jnp.bfloat16)
    image_handed_back = logit_scale * jnp.dot(pair_factor, text_embedding, preferred_element_type=jnp.float32)
    text_handed_back = logit_scale * jnp.dot(pair_factor.T, image_embedding, preferred_element_type=jnp.float32)
    text_grad_out = unit_backward(text_handed_back, text_unit, text_lengths).astype(jnp.bfloat16)
    grad_text = jnp.dot(text_pooled_features.T, text_grad_out, preferred_element_type=jnp.float32)
    text_feature_grad = jnp.dot(text_grad_out, text_head_weight.T, preferred_element_type=jnp.float32).astype(jnp.bfloat16)
    image_grad_out = unit_backward(image_handed_back, image_unit, image_lengths).astype(jnp.bfloat16)
    grad_out = jnp.dot(pooled.T, image_grad_out, preferred_element_type=jnp.float32)
    pooled_grad = jnp.dot(image_grad_out, output_weight.T, preferred_element_type=jnp.float32).astype(jnp.bfloat16)
    pooled_blocks = pooled_grad.reshape(IMAGES // B_DEV, B_DEV, HEADS, head_width)

    def backward(totals, inputs):
        image_batch, block_grad = inputs
        key_part, value_part, weights, weights_half = attend(image_batch, key_value_matrix, query_half, score_root)
        weight_grad = jnp.einsum('nhe,nphe->nhp', block_grad.astype(jnp.float32), value_part.astype(jnp.float32))
        score_grad = (weights * (weight_grad - lax.optimization_barrier(jnp.sum(weights * weight_grad, axis=-1, keepdims=True)))).astype(jnp.bfloat16)
        probe_term = jnp.einsum('nhp,nphe->he', score_grad.astype(jnp.float32), key_part.astype(jnp.float32)) / score_root
        key_grad = jnp.swapaxes(score_grad, 1, 2).astype(jnp.float32)[..., None] * query_half.astype(jnp.float32) / score_root
        value_grad = jnp.swapaxes(weights_half, 1, 2).astype(jnp.float32)[..., None] * block_grad.astype(jnp.float32)[:, None]
        kv_grad = jnp.stack([key_grad, value_grad], axis=2).astype(jnp.bfloat16).reshape(B_DEV * PATCH, 2 * D)
        kv_term = jnp.dot(image_batch.reshape(B_DEV * PATCH, D).T, kv_grad, preferred_element_type=jnp.float32)
        return ((totals[0] + kv_term, totals[1] + probe_term), None)
    start_totals = (jnp.zeros((D, 2 * D), jnp.float32), jnp.zeros((HEADS, head_width), jnp.float32))
    (grad_key_value, probe_total), _ = lax.scan(backward, start_totals, (image_blocks, pooled_blocks))
    return (grad_key_value, grad_out, grad_text, probe_total.reshape(D), text_feature_grad)
```

```python
import functools
import math

import jax
import jax.numpy as jnp
from jax import lax
from jax.experimental import pallas as pl
from jax.experimental.pallas import tpu as pltpu
from jax.sharding import PartitionSpec as P

HEADS = 16
D = 1152
HEAD = D // HEADS
PATCH = 32
ROWS = 16
NL = 16
NG = 8
SLAB = D // NL
OWN = SLAB // NG
ROOT = math.sqrt(HEAD)
MESH = pl.DeviceIdType.MESH
F32 = jnp.float32
BF16 = jnp.bfloat16


def nn(a, b):
    return lax.dot_general(a, b, (((1,), (0,)), ((), ())), preferred_element_type=F32)


def nt(a, b):
    return lax.dot_general(a, b, (((1,), (1,)), ((), ())), preferred_element_type=F32)


def flip(a):
    return a.astype(F32).T.astype(BF16)


def iota(shape, dim):
    return lax.broadcasted_iota(jnp.int32, shape, dim)


def slab_of(values, place):
    block, shift = divmod(SLAB * place, 128)
    first = values[:, 128 * block : 128 * block + 128]
    if shift == 0:
        return first
    first = pltpu.roll(first, 128 - shift, 1)
    if shift + SLAB <= 128:
        return first
    second = pltpu.roll(values[:, 128 * block + 128 : 128 * block + 256], 128 - shift, 1)
    return jnp.where(iota(first.shape, 1) < 128 - shift, first, second)


def send_all(axis, count, me, source, target, send_sem, recv_sem):
    def one(step, carry):
        peer = lax.rem(me + step, count)
        pltpu.make_async_remote_copy(
            src_ref=source(peer),
            dst_ref=target.at[me],
            send_sem=send_sem,
            recv_sem=recv_sem,
            device_id={axis: peer},
            device_id_type=MESH,
        ).start()
        return carry

    lax.fori_loop(1, count, one, 0)


def all_but_one(axis, count, me, target, send_sem, recv_sem):
    part = target.at[pl.ds(0, count - 1)]
    return pltpu.make_async_remote_copy(
        src_ref=part,
        dst_ref=part,
        send_sem=send_sem,
        recv_sem=recv_sem,
        device_id={axis: lax.rem(me + 1, count)},
        device_id_type=MESH,
    )


def slot_sum(ref, count):
    total = ref[0].astype(F32)
    for slot in range(1, count):
        total = total + ref[slot].astype(F32)
    return total


def unit_backward(gradient, unit, length):
    return (gradient - unit * jnp.sum(unit * gradient, axis=1, keepdims=True)) / length


def kernel(
    scale_ref,
    bias_ref,
    probe_ref,
    text_ref,
    x_hbm,
    wkv_hbm,
    wout_hbm,
    wtext_hbm,
    gkv_ref,
    gout_ref,
    gtext_ref,
    gprobe_ref,
    gfeat_ref,
    x_ref,
    wkv_ref,
    wout_ref,
    wtext_ref,
    kv_ref,
    mask_ref,
    soft_ref,
    texts,
    images,
    slab_out,
    slab_in,
    iret_out,
    iret_in,
    tret_out,
    tret_in,
    tgo_all,
    igo_all,
    small_out,
    small_in,
    last_out,
    last_in,
    tiny_in,
    probe_rows,
    part_ref,
    last_f32,
    pgt_ref,
    gvt_ref,
    load_sem,
    send_sem,
    recv_sem,
):
    l = lax.axis_index("loop")
    k = lax.axis_index("grp")

    loads = [
        pltpu.make_async_copy(wtext_hbm, wtext_ref, load_sem.at[0]),
        pltpu.make_async_copy(x_hbm, x_ref, load_sem.at[1]),
        pltpu.make_async_copy(wkv_hbm, wkv_ref, load_sem.at[2]),
        pltpu.make_async_copy(wout_hbm, wout_ref, load_sem.at[3]),
    ]
    for load in loads:
        load.start()

    barrier = pltpu.get_barrier_semaphore()

    def greet(axis, count, me):
        def one(step, carry):
            pl.semaphore_signal(
                barrier, inc=1, device_id={axis: lax.rem(me + step, count)}, device_id_type=MESH
            )
            return carry

        lax.fori_loop(1, count, one, 0)

    greet("loop", NL, l)
    greet("grp", NG, k)

    def send_loop(phase, source, target):
        send_all("loop", NL, l, source, target, send_sem.at[phase], recv_sem.at[phase])

    def send_grp(phase, source, target):
        send_all("grp", NG, k, source, target, send_sem.at[phase], recv_sem.at[phase])

    def loop_copies(phase, target):
        return all_but_one("loop", NL, l, target, send_sem.at[phase], recv_sem.at[phase])

    def grp_copies(phase, target):
        return all_but_one("grp", NG, k, target, send_sem.at[phase], recv_sem.at[phase])

    head_of_row = iota((NL * ROWS, D), 0) >> 4
    column = iota((NL * ROWS, D), 1)
    in_head = (column >= head_of_row * HEAD) & (column < head_of_row * HEAD + HEAD)
    mask_ref[...] = jnp.where(in_head, 1.0, 0.0).astype(BF16)

    text_rows = text_ref[...].astype(F32)
    for place in range(NL):
        slab_out[place, (HEADS + 1) * ROWS :, :] = slab_of(text_rows, place).astype(BF16)

    loads[0].wait()
    text_out = nn(text_ref[...], wtext_ref[...])
    text_length = jnp.sqrt(jnp.sum(text_out * text_out, axis=1, keepdims=True) + 1e-06)
    text_unit = text_out / text_length
    texts[l] = text_unit.astype(BF16)
    pl.semaphore_wait(barrier, NL + NG - 2)
    send_loop(0, lambda p: texts.at[l], texts)

    loads[1].wait()
    loads[2].wait()

    def project(step, carry):
        columns = pl.ds(pl.multiple_of(step * 256, 256), 256)
        kv_ref[:, columns] = nn(x_ref[...], wkv_ref[:, columns]).astype(BF16)
        return carry

    lax.fori_loop(0, 2 * D // 256, project, 0)

    query = probe_ref[...].astype(BF16).astype(F32)
    query_heads = (mask_ref[...].astype(F32) * query).astype(BF16)
    same = (iota((ROWS * PATCH, HEADS * ROWS), 0) >> 5) == (
        iota((ROWS * PATCH, HEADS * ROWS), 1) & (ROWS - 1)
    )
    scores = nt(kv_ref[:, :D], query_heads) / ROOT
    highest = jnp.max(jnp.where(same, scores, -jnp.inf), axis=0, keepdims=True)
    powers = jnp.where(same, jnp.exp(scores - highest), 0.0)
    weights = powers / jnp.sum(powers, axis=0, keepdims=True)
    soft_ref[...] = weights
    weights_t = weights.T.astype(BF16)

    mixed = nn(weights_t, kv_ref[:, D:]) * mask_ref[...].astype(F32)
    pooled = jnp.sum(mixed.reshape(HEADS, ROWS, D), axis=0)
    pooled_half = pooled.astype(BF16)
    loads[3].wait()
    image_out = nn(pooled_half, wout_ref[...])
    image_length = jnp.sqrt(jnp.sum(image_out * image_out, axis=1, keepdims=True) + 1e-06)
    image_unit = image_out / image_length
    images[k] = image_unit.astype(BF16)
    send_grp(1, lambda p: images.at[k], images)

    part_ref[...] = nn(weights_t, x_ref[...])
    pooled_rows = pooled_half.astype(F32)
    for place in range(NL):
        slab_out[place, : HEADS * ROWS, :] = slab_of(part_ref[...], place).astype(BF16)
        slab_out[place, HEADS * ROWS : (HEADS + 1) * ROWS, :] = slab_of(pooled_rows, place).astype(
            BF16
        )
    slab_in[l] = slab_out[l]

    temperature = jnp.exp(scale_ref[...])
    loop_copies(0, texts).wait_recv()
    grp_copies(1, images).wait_recv()
    text_all = texts[...].reshape(NL * ROWS, D)
    image_all = images[...].reshape(NG * ROWS, D)
    logits = temperature * nt(image_all, text_all) + bias_ref[...]
    row = iota((NG * ROWS, NL * ROWS), 0)
    col = iota((NG * ROWS, NL * ROWS), 1)
    matched = ((row >> 4) == k) & ((col >> 4) == l) & ((row & 15) == (col & 15))
    sign = jnp.where(matched, 1.0, -1.0)
    coeff = -sign / (1.0 + jnp.exp(sign * logits))
    tret_out[...] = nn(flip(coeff), image_all).astype(BF16).reshape(NL, ROWS, D)
    tret_in[l] = tret_out[l]
    send_loop(2, lambda p: tret_out.at[p], tret_in)
    iret_out[...] = nn(coeff.astype(BF16), text_all).astype(BF16).reshape(NG, ROWS, D)
    iret_in[k] = iret_out[k]
    send_grp(3, lambda p: iret_out.at[p], iret_in)
    send_loop(4, lambda p: slab_out.at[p], slab_in)

    grp_copies(3, iret_in).wait_recv()
    image_returned = temperature * slot_sum(iret_in, NG)
    image_grad = unit_backward(image_returned, image_unit, image_length).astype(BF16)
    igo_all[l] = image_grad
    send_loop(5, lambda p: igo_all.at[l], igo_all)

    loop_copies(2, tret_in).wait_recv()
    text_returned = temperature * slot_sum(tret_in, NL)
    text_grad = unit_backward(text_returned, text_unit, text_length).astype(BF16)
    tgo_all[l] = text_grad
    send_loop(6, lambda p: tgo_all.at[l], tgo_all)

    pooled_grad = nt(image_grad, wout_ref[...]).astype(BF16).astype(F32)
    tiled = jnp.concatenate([pooled_grad] * HEADS, axis=0)
    grad_heads = (mask_ref[...].astype(F32) * tiled).astype(BF16)
    weight_grad = nt(kv_ref[:, D:], grad_heads)
    weights = soft_ref[...]
    inner = jnp.sum(weights * weight_grad, axis=0, keepdims=True)
    score_grad = (weights * (weight_grad - inner)).astype(BF16)
    fold = jnp.where((iota((HEADS * ROWS, 128), 0) >> 4) == iota((HEADS * ROWS, 128), 1), 1.0, 0.0)
    score_grad_t = nn(score_grad, fold.astype(BF16)).T[:HEADS].astype(BF16)
    key_sum = nn(score_grad_t, x_ref[...])
    head_row = iota((HEADS, D), 0)
    head_col = iota((HEADS, D), 1)
    own_head = (head_col >= head_row * HEAD) & (head_col < head_row * HEAD + HEAD)
    probe_sum = nn(score_grad_t, kv_ref[:, :D])
    probe_sum = jnp.sum(jnp.where(own_head, probe_sum, 0.0), axis=0, keepdims=True) / ROOT
    probe_rows[...] = jnp.zeros_like(probe_rows)
    for block in range(D // 128):
        probe_rows[block : block + 1, :] = probe_sum[:, 128 * block : 128 * block + 128]
    for place in range(NL):
        small_out[place, :HEADS, :] = slab_of(key_sum, place)
        small_out[place, HEADS:, :] = probe_rows[...]
    small_in[l] = small_out[l]
    send_loop(7, lambda p: small_out.at[p], small_in)

    gfeat_ref[...] = nt(text_grad, wtext_ref[...]).astype(BF16)

    last_f32[...] = jnp.zeros_like(last_f32)

    def place_rows(offset):
        for part in range(NG):
            last_f32[32 * part + offset : 32 * part + offset + OWN, :] = part_ref[
                OWN * part : OWN * part + OWN, :
            ]

    loop_copies(4, slab_in).wait_recv()
    loop_copies(5, igo_all).wait_recv()
    igo = igo_all[...].reshape(NL * ROWS, D)
    pgt_ref[...] = nt(wout_ref[...], igo).astype(BF16).astype(F32)
    for head in range(HEADS):
        left = pgt_ref[HEAD * head : HEAD * head + HEAD, :].astype(BF16)
        right = slab_in[:, ROWS * head : ROWS * head + ROWS, :].reshape(NL * ROWS, 128)
        gvt_ref[HEAD * head : HEAD * head + HEAD, :] = nn(left, right)
    part_ref[:128, :] = gvt_ref[...].T
    place_rows(2 * OWN)
    pooled_slab = slab_in[:, HEADS * ROWS : (HEADS + 1) * ROWS, :].reshape(NL * ROWS, 128)
    part_ref[:128, :] = nn(flip(pooled_slab), igo)
    place_rows(OWN)
    loop_copies(6, tgo_all).wait_recv()
    tgo = tgo_all[...].reshape(NL * ROWS, D)
    text_slab = slab_in[:, (HEADS + 1) * ROWS :, :].reshape(NL * ROWS, 128)
    part_ref[:128, :] = nn(flip(text_slab), tgo)
    place_rows(0)
    last_out[...] = last_f32[...].astype(BF16).reshape(NG, 32, D)
    last_in[k] = last_out[k]
    send_grp(8, lambda p: last_out.at[p], last_in)

    loop_copies(7, small_in).wait_recv()
    tiny_in[k] = slot_sum(small_in, NL)
    send_grp(9, lambda p: tiny_in.at[k], tiny_in)

    grp_copies(9, tiny_in).wait_recv()
    tiny = slot_sum(tiny_in, NG)
    for block in range(D // 128):
        gprobe_ref[:, 128 * block : 128 * block + 128] = tiny[HEADS + block : HEADS + block + 1, :]
    own_columns = pltpu.roll(tiny[:HEADS, :], lax.rem(128 - OWN * k, 128), 1)
    key_grad = lax.dot_general(
        own_columns.T,
        jnp.where(own_head, query, 0.0) / ROOT,
        (((1,), (0,)), ((), ())),
        preferred_element_type=F32,
        precision=lax.Precision.HIGHEST,
    )
    gkv_ref[:, :D] = key_grad[:OWN]

    grp_copies(8, last_in).wait_recv()
    last_f32[:32, :] = slot_sum(last_in, NG)
    gtext_ref[...] = last_f32[:OWN, :]
    gout_ref[...] = last_f32[OWN : 2 * OWN, :]
    gkv_ref[:, D:] = last_f32[2 * OWN : 3 * OWN, :]

    for phase, target in ((0, texts), (2, tret_in), (4, slab_in), (5, igo_all), (6, tgo_all), (7, small_in)):
        loop_copies(phase, target).wait_send()
    for phase, target in ((1, images), (3, iret_in), (8, last_in), (9, tiny_in)):
        grp_copies(phase, target).wait_send()


def shards(patches, probe, key_value_matrix, output_weight, text, text_weight, log_scale, bias):
    vmem = pl.BlockSpec(memory_space=pltpu.VMEM)
    anywhere = pl.BlockSpec(memory_space=pl.ANY)
    slab_rows = (HEADS + 2) * ROWS
    outs = pl.pallas_call(
        kernel,
        out_shape=(
            jax.ShapeDtypeStruct((OWN, 2 * D), F32),
            jax.ShapeDtypeStruct((OWN, D), F32),
            jax.ShapeDtypeStruct((OWN, D), F32),
            jax.ShapeDtypeStruct((1, D), F32),
            jax.ShapeDtypeStruct((ROWS, D), BF16),
        ),
        in_specs=[vmem] * 4 + [anywhere] * 4,
        out_specs=(vmem,) * 5,
        scratch_shapes=[
            pltpu.VMEM((ROWS * PATCH, D), BF16),
            pltpu.VMEM((D, 2 * D), BF16),
            pltpu.VMEM((D, D), BF16),
            pltpu.VMEM((D, D), BF16),
            pltpu.VMEM((ROWS * PATCH, 2 * D), BF16),
            pltpu.VMEM((HEADS * ROWS, D), BF16),
            pltpu.VMEM((ROWS * PATCH, HEADS * ROWS), F32),
            pltpu.VMEM((NL, ROWS, D), BF16),
            pltpu.VMEM((NG, ROWS, D), BF16),
            pltpu.VMEM((NL, slab_rows, 128), BF16),
            pltpu.VMEM((NL, slab_rows, 128), BF16),
            pltpu.VMEM((NG, ROWS, D), BF16),
            pltpu.VMEM((NG, ROWS, D), BF16),
            pltpu.VMEM((NL, ROWS, D), BF16),
            pltpu.VMEM((NL, ROWS, D), BF16),
            pltpu.VMEM((NL, ROWS, D), BF16),
            pltpu.VMEM((NL, ROWS, D), BF16),
            pltpu.VMEM((NL, 2 * HEADS, 128), F32),
            pltpu.VMEM((NL, 2 * HEADS, 128), F32),
            pltpu.VMEM((NG, 32, D), BF16),
            pltpu.VMEM((NG, 32, D), BF16),
            pltpu.VMEM((NG, 2 * HEADS, 128), F32),
            pltpu.VMEM((HEADS, 128), F32),
            pltpu.VMEM((HEADS * ROWS, D), F32),
            pltpu.VMEM((NG * 32, D), F32),
            pltpu.VMEM((D, NL * ROWS), F32),
            pltpu.VMEM((D, 128), F32),
            pltpu.SemaphoreType.DMA((4,)),
            pltpu.SemaphoreType.DMA((10,)),
            pltpu.SemaphoreType.DMA((10,)),
        ],
        compiler_params=pltpu.CompilerParams(
            collective_id=0, has_side_effects=True, vmem_limit_bytes=56 * 1024 * 1024
        ),
    )(
        log_scale.reshape(1, 1),
        bias.reshape(1, 1),
        probe.reshape(1, D),
        text,
        patches.reshape(ROWS * PATCH, D),
        key_value_matrix,
        output_weight,
        text_weight,
    )
    return outs[0], outs[1], outs[2], outs[3].reshape(D), outs[4]


def solution(mesh):
    rows = P(("loop", "grp"), None)
    return jax.shard_map(
        shards,
        mesh=mesh,
        in_specs=(P(("loop", "grp"), None, None), P(), P(), P(), rows, P(), P(), P()),
        out_specs=(rows, rows, rows, P(), rows),
        check_vma=False,
    )
```

```python
import functools
import math

import jax
import jax.numpy as jnp
import ml_dtypes
import numpy as np
from jax import lax
from jax.experimental import pallas as pl
from jax.experimental.pallas import tpu as pltpu
from jax.sharding import PartitionSpec as P

HEADS = 16
D = 1152
HEAD = D // HEADS
PATCH = 32
ROWS = 16
NC = 8
NP = 16
SLAB = D // NC
OWN = SLAB // NP
SPARE = SLAB - 128
ROOT = math.sqrt(HEAD)
MESH = pl.DeviceIdType.MESH
F32 = jnp.float32
BF16 = jnp.bfloat16


def nn(a, b):
    return lax.dot_general(a, b, (((1,), (0,)), ((), ())), preferred_element_type=F32)


def nt(a, b):
    return lax.dot_general(a, b, (((1,), (1,)), ((), ())), preferred_element_type=F32)


def flip(a):
    return a.astype(F32).T.astype(BF16)


def iota(shape, dim):
    return lax.broadcasted_iota(jnp.int32, shape, dim)


def slab_of(values, start):
    block, shift = divmod(start, 128)
    first = values[:, 128 * block : 128 * block + 128]
    if shift == 0:
        return first
    first = pltpu.roll(first, 128 - shift, 1)
    if 128 * block + 128 >= values.shape[1]:
        return first
    second = pltpu.roll(values[:, 128 * block + 128 : 128 * block + 256], 128 - shift, 1)
    return jnp.where(iota(first.shape, 1) < 128 - shift, first, second)


def send_all(peer_of, count, me, source, target, send_sem, recv_sem):
    def one(step, carry):
        peer = lax.rem(me + step, count)
        pltpu.make_async_remote_copy(
            src_ref=source(peer),
            dst_ref=target(me),
            send_sem=send_sem,
            recv_sem=recv_sem,
            device_id=peer_of(peer),
            device_id_type=MESH,
        ).start()
        return carry

    lax.fori_loop(1, count, one, 0)


def all_but_one(peer_of, count, me, target, send_sem, recv_sem):
    part = target(pl.ds(0, count - 1))
    return pltpu.make_async_remote_copy(
        src_ref=part,
        dst_ref=part,
        send_sem=send_sem,
        recv_sem=recv_sem,
        device_id=peer_of(lax.rem(me + 1, count)),
        device_id_type=MESH,
    )


def slot_sum(ref, count):
    total = ref[0].astype(F32)
    for slot in range(1, count):
        total = total + ref[slot].astype(F32)
    return total


def unit_backward(gradient, unit, length):
    return (gradient - unit * jnp.sum(unit * gradient, axis=1, keepdims=True)) / length


def kernel(
    scale_ref,
    bias_ref,
    probe_ref,
    text_ref,
    x_hbm,
    wkv_hbm,
    wout_hbm,
    wtext_hbm,
    order_hbm,
    gkv_ref,
    gout_ref,
    gtext_ref,
    gprobe_ref,
    gfeat_ref,
    x_ref,
    wkv_ref,
    wout_ref,
    wtext_ref,
    order_ref,
    kv_ref,
    mask_ref,
    soft_ref,
    texts,
    images,
    slab_out,
    slab_in,
    iret_out,
    iret_in,
    tret_out,
    tret_in,
    tgo_all,
    igo_all,
    small_out,
    small_in,
    last_out,
    last_in,
    tiny_out,
    tiny_in,
    part_ref,
    last_f32,
    heads_ref,
    load_sem,
    send_sem,
    recv_sem,
):
    l = lax.axis_index("loop")
    k = lax.axis_index("grp")
    c = (k % 2) * 4 + l % 4
    s = (l // 4) * 4 + k // 2

    def in_column(peer):
        return {"loop": (l // 4) * 4 + peer % 4, "grp": (k // 2) * 2 + peer // 4}

    def in_plane(peer):
        return {"loop": (peer // 4) * 4 + l % 4, "grp": (peer % 4) * 2 + k % 2}

    loads = [
        pltpu.make_async_copy(wtext_hbm, wtext_ref, load_sem.at[0]),
        pltpu.make_async_copy(x_hbm, x_ref, load_sem.at[1]),
        pltpu.make_async_copy(wkv_hbm, wkv_ref, load_sem.at[2]),
        pltpu.make_async_copy(wout_hbm, wout_ref, load_sem.at[3]),
        pltpu.make_async_copy(order_hbm, order_ref, load_sem.at[4]),
    ]
    for load in loads:
        load.start()

    barrier = pltpu.get_barrier_semaphore()

    def greet(peer_of, count, me):
        def one(step, carry):
            peer = peer_of(lax.rem(me + step, count))
            pl.semaphore_signal(barrier, inc=1, device_id=peer, device_id_type=MESH)
            return carry

        lax.fori_loop(1, count, one, 0)

    greet(in_plane, NP, s)
    greet(in_column, NC, c)

    column = (in_column, NC, c)
    plane = (in_plane, NP, s)
    phases = {
        0: (plane, lambda i: texts.at[i]),
        1: (column, lambda i: images.at[i]),
        2: (plane, lambda i: tret_in.at[i]),
        3: (column, lambda i: iret_in.at[i]),
        4: (column, lambda i: slab_in.at[i]),
        5: (column, lambda i: igo_all.at[i]),
        6: (column, lambda i: tgo_all.at[i]),
        7: (column, lambda i: small_in.at[i]),
        8: (plane, lambda i: last_in.at[0, i]),
        9: (plane, lambda i: last_in.at[1, i]),
        10: (plane, lambda i: tiny_in.at[i]),
    }
    started = []

    def copies(phase):
        (peer_of, count, me), target = phases[phase]
        return all_but_one(peer_of, count, me, target, send_sem.at[phase], recv_sem.at[phase])

    def send(phase, source):
        (peer_of, count, me), target = phases[phase]
        send_all(peer_of, count, me, source, target, send_sem.at[phase], recv_sem.at[phase])
        started.append(phase)

    def arrive(phase):
        copies(phase).wait_recv()

    head_of_row = iota((HEADS * ROWS, D), 0) >> 4
    lane = iota((HEADS * ROWS, D), 1)
    in_head = (lane >= head_of_row * HEAD) & (lane < head_of_row * HEAD + HEAD)
    mask_ref[...] = jnp.where(in_head, 1.0, 0.0).astype(BF16)

    loads[0].wait()
    text_out = nn(text_ref[...], wtext_ref[...])
    text_length = jnp.sqrt(jnp.sum(text_out * text_out, axis=1, keepdims=True) + 1e-06)
    text_unit = text_out / text_length
    texts[s] = text_unit.astype(BF16)
    pl.semaphore_wait(barrier, NP + NC - 2)
    send(0, lambda p: texts.at[s])

    loads[1].wait()
    loads[2].wait()

    def project(step, carry):
        columns = pl.ds(pl.multiple_of(step * 256, 256), 256)
        kv_ref[:, columns] = nn(x_ref[...], wkv_ref[:, columns]).astype(BF16)
        return carry

    lax.fori_loop(0, 2 * D // 256, project, 0)

    query = probe_ref[...].astype(BF16).astype(F32)
    query_heads = (mask_ref[...].astype(F32) * query).astype(BF16)
    same = (iota((ROWS * PATCH, HEADS * ROWS), 0) >> 5) == (
        iota((ROWS * PATCH, HEADS * ROWS), 1) & (ROWS - 1)
    )
    scores = nt(kv_ref[:, :D], query_heads) / ROOT
    highest = jnp.max(jnp.where(same, scores, -jnp.inf), axis=0, keepdims=True)
    powers = jnp.where(same, jnp.exp(scores - highest), 0.0)
    weights = powers / jnp.sum(powers, axis=0, keepdims=True)
    soft_ref[...] = weights
    weights_t = weights.T.astype(BF16)

    mixed = nn(weights_t, kv_ref[:, D:]) * mask_ref[...].astype(F32)
    pooled = jnp.sum(mixed.reshape(HEADS, ROWS, D), axis=0)
    pooled_half = pooled.astype(BF16)
    loads[3].wait()
    image_out = nn(pooled_half, wout_ref[...])
    image_length = jnp.sqrt(jnp.sum(image_out * image_out, axis=1, keepdims=True) + 1e-06)
    image_unit = image_out / image_length
    images[c] = image_unit.astype(BF16)
    send(1, lambda p: images.at[c])

    patch_sums = nn(weights_t, x_ref[...]).astype(BF16)
    features = jnp.concatenate([pooled_half, text_ref[...]], axis=0)
    loads[4].wait()

    for place in range(NC):
        rows = order_ref[SLAB * place : SLAB * place + SLAB, :]
        slab_out[place, :SLAB, :] = nt(rows, patch_sums).astype(BF16)
        slab_out[place, SLAB:, :SLAB] = nt(features, rows).astype(BF16)
    slab_in[c] = slab_out[c]

    temperature = jnp.exp(scale_ref[...])
    arrive(0)
    arrive(1)
    text_all = texts[...].reshape(NP * ROWS, D)
    image_all = images[...].reshape(NC * ROWS, D)
    logits = temperature * nt(image_all, text_all) + bias_ref[...]
    row = iota((NC * ROWS, NP * ROWS), 0)
    col = iota((NC * ROWS, NP * ROWS), 1)
    matched = ((row >> 4) == c) & ((col >> 4) == s) & ((row & 15) == (col & 15))
    sign = jnp.where(matched, 1.0, -1.0)
    coeff = -sign / (1.0 + jnp.exp(sign * logits))
    tret_out[...] = nn(flip(coeff), image_all).astype(BF16).reshape(NP, ROWS, D)
    tret_in[s] = tret_out[s]
    send(2, lambda p: tret_out.at[p])
    iret_out[...] = nn(coeff.astype(BF16), text_all).astype(BF16).reshape(NC, ROWS, D)
    iret_in[c] = iret_out[c]
    send(3, lambda p: iret_out.at[p])
    send(4, lambda p: slab_out.at[p])

    arrive(3)
    image_returned = temperature * slot_sum(iret_in, NC)
    image_grad = unit_backward(image_returned, image_unit, image_length).astype(BF16)
    igo_all[c] = image_grad
    send(5, lambda p: igo_all.at[c])

    pooled_grad = nt(image_grad, wout_ref[...]).astype(BF16).astype(F32)
    tiled = jnp.concatenate([pooled_grad] * HEADS, axis=0)
    grad_heads = (mask_ref[...].astype(F32) * tiled).astype(BF16)
    weight_grad = nt(kv_ref[:, D:], grad_heads)
    weights = soft_ref[...]
    inner = jnp.sum(weights * weight_grad, axis=0, keepdims=True)
    score_grad = (weights * (weight_grad - inner)).astype(BF16)
    fold = jnp.where((iota((HEADS * ROWS, 128), 0) >> 4) == iota((HEADS * ROWS, 128), 1), 1.0, 0.0)
    score_grad_t = nn(score_grad, fold.astype(BF16)).T[:HEADS].astype(BF16)

    key_sum = nn(score_grad_t, x_ref[...])
    high = key_sum.astype(BF16)
    low = (key_sum - high.astype(F32)).astype(BF16)
    key_sum = jnp.concatenate([high, low], axis=0)
    head_row = iota((HEADS, D), 0)
    head_col = iota((HEADS, D), 1)
    own_head = (head_col >= head_row * HEAD) & (head_col < head_row * HEAD + HEAD)
    probe_sum = jnp.where(own_head, nn(score_grad_t, kv_ref[:, :D]), 0.0) / ROOT
    tile_row = iota((HEADS, 128), 0)
    tile_lane = iota((HEADS, 128), 1)
    probe_tile = jnp.zeros((HEADS, 128), F32)
    for head in range(HEADS):
        probe_tile = jnp.where(tile_row == head, slab_of(probe_sum, HEAD * head), probe_tile)
    probe_tile = pltpu.roll(probe_tile, SPARE, 1)
    for place in range(NC):
        rows = order_ref[SLAB * place : SLAB * place + SLAB, :]
        split = nt(key_sum, rows)
        small_out[place, :, :SLAB] = split[:HEADS] + split[HEADS:]
        small_out[place, :, 128:] = jnp.where(
            tile_lane < SPARE, small_out[place, :, 128:], probe_tile
        )
    small_in[c] = small_out[c]
    send(7, lambda p: small_out.at[p])

    arrive(2)
    text_returned = temperature * slot_sum(tret_in, NP)
    text_grad = unit_backward(text_returned, text_unit, text_length).astype(BF16)
    tgo_all[c] = text_grad
    send(6, lambda p: tgo_all.at[c])

    last_f32[...] = jnp.zeros_like(last_f32)

    def place_rows(offset):
        for part in range(NP):
            last_f32[32 * part + offset : 32 * part + offset + OWN, :] = part_ref[
                OWN * part : OWN * part + OWN, :
            ]

    arrive(4)
    arrive(5)
    igo = igo_all[...].reshape(NC * ROWS, D)
    part_ref[...] = nn(flip(slab_in[:, SLAB : SLAB + ROWS, :].reshape(NC * ROWS, 256))[:SLAB], igo)
    place_rows(0)
    pooled_grads = nt(igo, wout_ref[...]).astype(BF16)
    for place in range(NC):
        tiled = jnp.concatenate([pooled_grads[ROWS * place : ROWS * place + ROWS]] * HEADS, axis=0)
        heads_ref[256 * place : 256 * place + 256, :] = mask_ref[...] * tiled
    left = jnp.concatenate([slab_in[place, :SLAB, :] for place in range(NC)], axis=1)
    part_ref[...] = nn(left, heads_ref[...])
    place_rows(OWN)

    def pack(half):
        rows = last_f32[...].reshape(NP, 32, D)[:, 16 * half : 16 * half + 16]
        last_out[half] = rows.astype(BF16)
        last_in[half, s] = last_out[half, s]

    pack(0)
    send(8, lambda p: last_out.at[0, p])

    arrive(7)
    tiny = slot_sum(small_in, NC)
    for place in range(NP):
        tiny_out[place] = jnp.where(
            tile_lane < SPARE, slab_of(tiny, OWN * place), tiny[:, 128:]
        )
    tiny_in[s] = tiny_out[s]
    send(10, lambda p: tiny_out.at[p])

    arrive(6)
    tgo = tgo_all[...].reshape(NC * ROWS, D)
    part_ref[...] = nn(flip(slab_in[:, SLAB + ROWS :, :].reshape(NC * ROWS, 256))[:SLAB], tgo)
    place_rows(2 * OWN)
    pack(1)
    send(9, lambda p: last_out.at[1, p])

    gfeat_ref[...] = nt(text_grad, wtext_ref[...]).astype(BF16)

    arrive(10)
    tiny = slot_sum(tiny_in, NP)
    gprobe_ref[...] = pltpu.roll(tiny, 128 - SPARE, 1)[:, :HEAD]
    key_grad = lax.dot_general(
        tiny.T[:16, :],
        jnp.where(own_head, query, 0.0) / ROOT,
        (((1,), (0,)), ((), ())),
        preferred_element_type=F32,
        precision=lax.Precision.HIGHEST,
    )
    gkv_ref[:, :D] = key_grad[:OWN]

    arrive(8)
    last_f32[:16, :] = slot_sum(last_in.at[0], NP)
    arrive(9)
    last_f32[16:32, :] = slot_sum(last_in.at[1], NP)
    gout_ref[...] = last_f32[:OWN, :]
    gkv_ref[:, D:] = last_f32[OWN : 2 * OWN, :]
    gtext_ref[...] = last_f32[2 * OWN : 3 * OWN, :]

    for phase in started:
        copies(phase).wait_send()


def column_order():
    c, s, r = np.meshgrid(np.arange(NC), np.arange(NP), np.arange(OWN), indexing="ij")
    loop = (s // 4) * 4 + c % 4
    grp = (s % 4) * 2 + c // 4
    kept = ((loop * 8 + grp) * OWN + r).reshape(D)
    return (kept[:, None] == np.arange(D)[None, :]).astype(ml_dtypes.bfloat16)


def shards(patches, probe, key_value_matrix, output_weight, text, text_weight, log_scale, bias):
    vmem = pl.BlockSpec(memory_space=pltpu.VMEM)
    anywhere = pl.BlockSpec(memory_space=pl.ANY)
    outs = pl.pallas_call(
        kernel,
        out_shape=(
            jax.ShapeDtypeStruct((OWN, 2 * D), F32),
            jax.ShapeDtypeStruct((OWN, D), F32),
            jax.ShapeDtypeStruct((OWN, D), F32),
            jax.ShapeDtypeStruct((HEADS, HEAD), F32),
            jax.ShapeDtypeStruct((ROWS, D), BF16),
        ),
        in_specs=[vmem] * 4 + [anywhere] * 5,
        out_specs=(vmem,) * 5,
        scratch_shapes=[
            pltpu.VMEM((ROWS * PATCH, D), BF16),
            pltpu.VMEM((D, 2 * D), BF16),
            pltpu.VMEM((D, D), BF16),
            pltpu.VMEM((D, D), BF16),
            pltpu.VMEM((D, D), BF16),
            pltpu.VMEM((ROWS * PATCH, 2 * D), BF16),
            pltpu.VMEM((HEADS * ROWS, D), BF16),
            pltpu.VMEM((ROWS * PATCH, HEADS * ROWS), F32),
            pltpu.VMEM((NP, ROWS, D), BF16),
            pltpu.VMEM((NC, ROWS, D), BF16),
            pltpu.VMEM((NC, SLAB + 2 * ROWS, HEADS * ROWS), BF16),
            pltpu.VMEM((NC, SLAB + 2 * ROWS, HEADS * ROWS), BF16),
            pltpu.VMEM((NC, ROWS, D), BF16),
            pltpu.VMEM((NC, ROWS, D), BF16),
            pltpu.VMEM((NP, ROWS, D), BF16),
            pltpu.VMEM((NP, ROWS, D), BF16),
            pltpu.VMEM((NC, ROWS, D), BF16),
            pltpu.VMEM((NC, ROWS, D), BF16),
            pltpu.VMEM((NC, HEADS, 256), F32),
            pltpu.VMEM((NC, HEADS, 256), F32),
            pltpu.VMEM((2, NP, 16, D), BF16),
            pltpu.VMEM((2, NP, 16, D), BF16),
            pltpu.VMEM((NP, HEADS, 128), F32),
            pltpu.VMEM((NP, HEADS, 128), F32),
            pltpu.VMEM((SLAB, D), F32),
            pltpu.VMEM((NP * 32, D), F32),
            pltpu.VMEM((NC * HEADS * ROWS, D), BF16),
            pltpu.SemaphoreType.DMA((5,)),
            pltpu.SemaphoreType.DMA((11,)),
            pltpu.SemaphoreType.DMA((11,)),
        ],
        compiler_params=pltpu.CompilerParams(
            collective_id=0, has_side_effects=True, vmem_limit_bytes=56 * 1024 * 1024
        ),
    )(
        log_scale.reshape(1, 1),
        bias.reshape(1, 1),
        probe.reshape(1, D),
        text,
        patches.reshape(ROWS * PATCH, D),
        key_value_matrix,
        output_weight,
        text_weight,
        jnp.asarray(column_order()),
    )
    return outs[0], outs[1], outs[2], outs[3].reshape(D), outs[4]


def solution(mesh):
    rows = P(("loop", "grp"), None)
    return jax.shard_map(
        shards,
        mesh=mesh,
        in_specs=(P(("loop", "grp"), None, None), P(), P(), P(), rows, P(), P(), P()),
        out_specs=(rows, rows, rows, P(), rows),
        check_vma=False,
    )
```

```python
import functools
import math

import jax
import jax.numpy as jnp
import ml_dtypes
import numpy as np
from jax import lax
from jax.experimental import pallas as pl
from jax.experimental.pallas import tpu as pltpu
from jax.sharding import PartitionSpec as P

HEADS = 16
D = 1152
HEAD = D // HEADS
PATCH = 32
ROWS = 16
NC = 8
NP = 16
SLAB = D // NC
OWN = SLAB // NP
SPARE = SLAB - 128
ROOT = math.sqrt(HEAD)
MESH = pl.DeviceIdType.MESH
F32 = jnp.float32
BF16 = jnp.bfloat16


def nn(a, b):
    return lax.dot_general(a, b, (((1,), (0,)), ((), ())), preferred_element_type=F32)


def nt(a, b):
    return lax.dot_general(a, b, (((1,), (1,)), ((), ())), preferred_element_type=F32)


def flip(a):
    return a.astype(F32).T.astype(BF16)


def exact(a, b):
    return lax.dot_general(
        a,
        b,
        (((1,), (0,)), ((), ())),
        preferred_element_type=F32,
        precision=lax.Precision.HIGHEST,
    )


def iota(shape, dim):
    return lax.broadcasted_iota(jnp.int32, shape, dim)


def slab_of(values, start):
    block, shift = divmod(start, 128)
    first = values[:, 128 * block : 128 * block + 128]
    if shift == 0:
        return first
    first = pltpu.roll(first, 128 - shift, 1)
    if 128 * block + 128 >= values.shape[1]:
        return first
    second = pltpu.roll(values[:, 128 * block + 128 : 128 * block + 256], 128 - shift, 1)
    return jnp.where(iota(first.shape, 1) < 128 - shift, first, second)


def send_all(peer_of, count, me, source, target, send_sem, recv_sem):
    def one(step, carry):
        peer = lax.rem(me + step, count)
        pltpu.make_async_remote_copy(
            src_ref=source(peer),
            dst_ref=target(me),
            send_sem=send_sem,
            recv_sem=recv_sem,
            device_id=peer_of(peer),
            device_id_type=MESH,
        ).start()
        return carry

    lax.fori_loop(1, count, one, 0)


def all_but_one(peer_of, count, me, target, send_sem, recv_sem):
    part = target(pl.ds(0, count - 1))
    return pltpu.make_async_remote_copy(
        src_ref=part,
        dst_ref=part,
        send_sem=send_sem,
        recv_sem=recv_sem,
        device_id=peer_of(lax.rem(me + 1, count)),
        device_id_type=MESH,
    )


def slot_sum(ref, count):
    total = ref[0].astype(F32)
    for slot in range(1, count):
        total = total + ref[slot].astype(F32)
    return total


def unit_backward(gradient, unit, length):
    return (gradient - unit * jnp.sum(unit * gradient, axis=1, keepdims=True)) / length


def kernel(
    scale_ref,
    bias_ref,
    probe_ref,
    text_ref,
    x_hbm,
    wkv_hbm,
    wout_hbm,
    wtext_hbm,
    order_hbm,
    sums_ref,
    gfeat_ref,
    x_ref,
    wk_ref,
    keys_ref,
    wv_ref,
    wout_ref,
    wtext_ref,
    order_ref,
    mask_ref,
    soft_ref,
    texts,
    images,
    slab_out,
    slab_in,
    iret_out,
    iret_in,
    tret_out,
    tret_in,
    tgo_all,
    igo_all,
    small_out,
    small_in,
    last_out,
    last_in,
    tiny_out,
    tiny_in,
    part_ref,
    last_f32,
    heads_ref,
    load_sem,
    send_sem,
    recv_sem,
):
    l = lax.axis_index("loop")
    k = lax.axis_index("grp")
    c = (k % 2) * 4 + l % 4
    s = (l // 4) * 4 + k // 2

    def in_column(peer):
        return {"loop": (l // 4) * 4 + peer % 4, "grp": (k // 2) * 2 + peer // 4}

    def in_plane(peer):
        return {"loop": (peer // 4) * 4 + l % 4, "grp": (peer % 4) * 2 + k % 2}

    def load(source, target, number):
        return pltpu.make_async_copy(source, target, load_sem.at[number])

    loads = [
        load(wtext_hbm, wtext_ref, 0),
        load(wkv_hbm.at[:, :D], wk_ref, 1),
        load(x_hbm, x_ref, 2),
        load(wkv_hbm.at[:, D:], wv_ref, 3),
        load(wout_hbm, wout_ref, 4),
        load(order_hbm, order_ref, 5),
    ]
    for number in range(3):
        loads[number].start()

    barrier = pltpu.get_barrier_semaphore()

    def greet(peer_of, count, me):
        def one(step, carry):
            peer = peer_of(lax.rem(me + step, count))
            pl.semaphore_signal(barrier, inc=1, device_id=peer, device_id_type=MESH)
            return carry

        lax.fori_loop(1, count, one, 0)

    greet(in_plane, NP, s)
    greet(in_column, NC, c)

    column = (in_column, NC, c)
    plane = (in_plane, NP, s)
    phases = {
        0: (plane, lambda i: texts.at[i]),
        1: (column, lambda i: images.at[i]),
        2: (plane, lambda i: tret_in.at[i]),
        3: (column, lambda i: iret_in.at[i]),
        4: (column, lambda i: slab_in.at[i]),
        5: (column, lambda i: igo_all.at[i]),
        6: (column, lambda i: tgo_all.at[i]),
        7: (column, lambda i: small_in.at[i]),
        8: (plane, lambda i: last_in.at[0, i]),
        9: (plane, lambda i: last_in.at[1, i]),
        10: (plane, lambda i: tiny_in.at[i]),
    }
    started = []

    def copies(phase):
        (peer_of, count, me), target = phases[phase]
        return all_but_one(peer_of, count, me, target, send_sem.at[phase], recv_sem.at[phase])

    def send(phase, source):
        (peer_of, count, me), target = phases[phase]
        send_all(peer_of, count, me, source, target, send_sem.at[phase], recv_sem.at[phase])
        started.append(phase)

    def arrive(phase):
        copies(phase).wait_recv()

    for number in range(3, 6):
        loads[number].start()

    head_of_row = iota((HEADS * ROWS, D), 0) >> 4
    lane = iota((HEADS * ROWS, D), 1)
    in_head = (lane >= head_of_row * HEAD) & (lane < head_of_row * HEAD + HEAD)
    mask_ref[...] = jnp.where(in_head, 1.0, 0.0).astype(BF16)

    loads[0].wait()
    text_out = nn(text_ref[...], wtext_ref[...])
    text_length = jnp.sqrt(jnp.sum(text_out * text_out, axis=1, keepdims=True) + 1e-06)
    text_unit = text_out / text_length
    texts[s] = text_unit.astype(BF16)
    pl.semaphore_wait(barrier, NP + NC - 2)
    send(0, lambda p: texts.at[s])

    query = probe_ref[...].reshape(1, D).astype(BF16).astype(F32)
    query_heads = (mask_ref[...].astype(F32) * query).astype(BF16)
    loads[1].wait()
    loads[2].wait()
    for block in range(3):
        columns = slice(384 * block, 384 * block + 384)
        keys_ref[:, columns] = nn(x_ref[...], wk_ref[:, columns]).astype(BF16)
    scores = nt(keys_ref[...], query_heads) / ROOT

    same = (iota((ROWS * PATCH, HEADS * ROWS), 0) >> 5) == (
        iota((ROWS * PATCH, HEADS * ROWS), 1) & (ROWS - 1)
    )
    highest = jnp.max(jnp.where(same, scores, -jnp.inf), axis=0, keepdims=True)
    powers = jnp.where(same, jnp.exp(scores - highest), 0.0)
    weights = powers / jnp.sum(powers, axis=0, keepdims=True)
    soft_ref[...] = weights
    weights_t = weights.T.astype(BF16)

    patch_sums = nn(weights_t, x_ref[...]).astype(BF16)
    loads[3].wait()
    mixed = nn(patch_sums, wv_ref[...]) * mask_ref[...].astype(F32)
    pooled = jnp.sum(mixed.reshape(HEADS, ROWS, D), axis=0)
    pooled_half = pooled.astype(BF16)
    loads[4].wait()
    image_out = nn(pooled_half, wout_ref[...])
    image_length = jnp.sqrt(jnp.sum(image_out * image_out, axis=1, keepdims=True) + 1e-06)
    image_unit = image_out / image_length
    images[c] = image_unit.astype(BF16)
    send(1, lambda p: images.at[c])

    features = jnp.concatenate([pooled_half, text_ref[...]], axis=0)
    loads[5].wait()
    for place in range(NC):
        rows = order_ref[SLAB * place : SLAB * place + SLAB, :]
        slab_out[place, :SLAB, :] = nt(rows, patch_sums).astype(BF16)
        slab_out[place, SLAB:, :SLAB] = nt(features, rows).astype(BF16)
    slab_in[c] = slab_out[c]
    send(4, lambda p: slab_out.at[p])

    temperature = jnp.exp(scale_ref[...])
    arrive(0)
    arrive(1)
    text_all = texts[...].reshape(NP * ROWS, D)
    image_all = images[...].reshape(NC * ROWS, D)
    logits = temperature * nt(image_all, text_all) + bias_ref[...]
    row = iota((NC * ROWS, NP * ROWS), 0)
    col = iota((NC * ROWS, NP * ROWS), 1)
    matched = ((row >> 4) == c) & ((col >> 4) == s) & ((row & 15) == (col & 15))
    sign = jnp.where(matched, 1.0, -1.0)
    coeff = -sign / (1.0 + jnp.exp(sign * logits))
    tret_out[...] = nn(flip(coeff), image_all).astype(BF16).reshape(NP, ROWS, D)
    tret_in[s] = tret_out[s]
    send(2, lambda p: tret_out.at[p])
    iret_out[...] = nn(coeff.astype(BF16), text_all).astype(BF16).reshape(NC, ROWS, D)
    iret_in[c] = iret_out[c]
    send(3, lambda p: iret_out.at[p])

    arrive(3)
    image_returned = temperature * slot_sum(iret_in, NC)
    image_grad = unit_backward(image_returned, image_unit, image_length).astype(BF16)
    igo_all[c] = image_grad
    send(5, lambda p: igo_all.at[c])

    pooled_grad = nt(image_grad, wout_ref[...]).astype(BF16).astype(F32)
    tiled = jnp.concatenate([pooled_grad] * HEADS, axis=0)
    grad_heads = (mask_ref[...].astype(F32) * tiled).astype(BF16)
    weight_grad = nn(x_ref[...], nt(wv_ref[...], grad_heads).astype(BF16))
    weights = soft_ref[...]
    inner = jnp.sum(weights * weight_grad, axis=0, keepdims=True)
    score_grad = (weights * (weight_grad - inner)).astype(BF16)
    fold = jnp.where((iota((HEADS * ROWS, 128), 0) >> 4) == iota((HEADS * ROWS, 128), 1), 1.0, 0.0)
    score_grad_t = nn(score_grad, fold.astype(BF16)).T[:HEADS].astype(BF16)

    key_sum = nn(score_grad_t, x_ref[...])
    high = key_sum.astype(BF16)
    low = (key_sum - high.astype(F32)).astype(BF16)
    key_sum = jnp.concatenate([high, low], axis=0)
    head_row = iota((HEADS, D), 0)
    head_col = iota((HEADS, D), 1)
    own_head = (head_col >= head_row * HEAD) & (head_col < head_row * HEAD + HEAD)
    probe_sum = jnp.where(own_head, nn(score_grad_t, keys_ref[...]), 0.0) / ROOT
    tile_row = iota((HEADS, 128), 0)
    tile_lane = iota((HEADS, 128), 1)
    probe_tile = jnp.zeros((HEADS, 128), F32)
    for head in range(HEADS):
        probe_tile = jnp.where(tile_row == head, slab_of(probe_sum, HEAD * head), probe_tile)
    probe_tile = pltpu.roll(probe_tile, SPARE, 1)
    for place in range(NC):
        rows = order_ref[SLAB * place : SLAB * place + SLAB, :]
        split = nt(key_sum, rows)
        small_out[place, :, :SLAB] = split[:HEADS] + split[HEADS:]
        small_out[place, :, 128:] = jnp.where(
            tile_lane < SPARE, small_out[place, :, 128:], probe_tile
        )
    small_in[c] = small_out[c]
    send(7, lambda p: small_out.at[p])

    arrive(2)
    text_returned = temperature * slot_sum(tret_in, NP)
    text_grad = unit_backward(text_returned, text_unit, text_length).astype(BF16)
    tgo_all[c] = text_grad
    send(6, lambda p: tgo_all.at[c])

    last_f32[...] = jnp.zeros_like(last_f32)

    def place_rows(offset):
        for part in range(NP):
            last_f32[32 * part + offset : 32 * part + offset + OWN, :] = part_ref[
                OWN * part : OWN * part + OWN, :
            ]

    arrive(4)
    arrive(5)
    igo = igo_all[...].reshape(NC * ROWS, D)
    part_ref[...] = nn(flip(slab_in[:, SLAB : SLAB + ROWS, :].reshape(NC * ROWS, 256))[:SLAB], igo)
    place_rows(0)
    pooled_grads = nt(igo, wout_ref[...]).astype(BF16)
    for place in range(NC):
        tiled = jnp.concatenate([pooled_grads[ROWS * place : ROWS * place + ROWS]] * HEADS, axis=0)
        heads_ref[256 * place : 256 * place + 256, :] = mask_ref[...] * tiled
    left = jnp.concatenate([slab_in[place, :SLAB, :] for place in range(NC)], axis=1)
    part_ref[...] = nn(left, heads_ref[...])
    place_rows(OWN)

    def pack(half):
        rows = last_f32[...].reshape(NP, 32, D)[:, 16 * half : 16 * half + 16]
        last_out[half] = rows.astype(BF16)
        last_in[half, s] = last_out[half, s]

    pack(0)
    send(8, lambda p: last_out.at[0, p])

    arrive(7)
    tiny = slot_sum(small_in, NC)
    for place in range(NP):
        tiny_out[place] = jnp.where(
            tile_lane < SPARE, slab_of(tiny, OWN * place), tiny[:, 128:]
        )
    tiny_in[s] = tiny_out[s]
    send(10, lambda p: tiny_out.at[p])

    arrive(6)
    tgo = tgo_all[...].reshape(NC * ROWS, D)
    part_ref[...] = nn(flip(slab_in[:, SLAB + ROWS :, :].reshape(NC * ROWS, 256))[:SLAB], tgo)
    place_rows(2 * OWN)
    pack(1)
    send(9, lambda p: last_out.at[1, p])

    gfeat_ref[...] = nt(text_grad, wtext_ref[...]).astype(BF16)

    arrive(10)
    tiny = slot_sum(tiny_in, NP)
    probe_tile = pltpu.roll(tiny, 128 - SPARE, 1)
    spread = jnp.where(iota((128, D), 0) == iota((1, D), 1) % HEAD, 1.0, 0.0)
    probe_grad = exact(probe_tile, spread)
    sums_ref[48:56, :] = jnp.broadcast_to(
        jnp.sum(jnp.where(own_head, probe_grad, 0.0), axis=0, keepdims=True), (8, D)
    )
    sums_ref[32:48, :] = exact(tiny.T[:16, :], jnp.where(own_head, query, 0.0) / ROOT)

    arrive(8)
    sums_ref[:16, :] = slot_sum(last_in.at[0], NP)
    arrive(9)
    sums_ref[16:32, :] = slot_sum(last_in.at[1], NP)

    for phase in started:
        copies(phase).wait_send()


def part_sums(sums_ref, feat_ref, gkv_ref, gout_ref, gtext_ref, gprobe_ref, gfeat_ref):
    gout_ref[...] = sums_ref[:OWN, :]
    gkv_ref[:, :D] = sums_ref[32 : 32 + OWN, :]
    gkv_ref[:, D:] = sums_ref[OWN : 2 * OWN, :]
    gtext_ref[...] = sums_ref[2 * OWN : 3 * OWN, :]
    gprobe_ref[...] = sums_ref[48:49, :].reshape(D)
    gfeat_ref[...] = feat_ref[...]


def column_order():
    c, s, r = np.meshgrid(np.arange(NC), np.arange(NP), np.arange(OWN), indexing="ij")
    loop = (s // 4) * 4 + c % 4
    grp = (s % 4) * 2 + c // 4
    kept = ((loop * 8 + grp) * OWN + r).reshape(D)
    return (kept[:, None] == np.arange(D)[None, :]).astype(ml_dtypes.bfloat16)


def shards(patches, probe, key_value_matrix, output_weight, text, text_weight, log_scale, bias):
    vmem = pl.BlockSpec(memory_space=pltpu.VMEM)
    anywhere = pl.BlockSpec(memory_space=pl.ANY)
    sums = pl.pallas_call(
        kernel,
        out_shape=(
            jax.ShapeDtypeStruct((56, D), F32),
            jax.ShapeDtypeStruct((ROWS, D), BF16),
        ),
        in_specs=[vmem] * 4 + [anywhere] * 5,
        out_specs=(vmem,) * 2,
        scratch_shapes=[
            pltpu.VMEM((ROWS * PATCH, D), BF16),
            pltpu.VMEM((D, D), BF16),
            pltpu.VMEM((ROWS * PATCH, D), BF16),
            pltpu.VMEM((D, D), BF16),
            pltpu.VMEM((D, D), BF16),
            pltpu.VMEM((D, D), BF16),
            pltpu.VMEM((D, D), BF16),
            pltpu.VMEM((HEADS * ROWS, D), BF16),
            pltpu.VMEM((ROWS * PATCH, HEADS * ROWS), F32),
            pltpu.VMEM((NP, ROWS, D), BF16),
            pltpu.VMEM((NC, ROWS, D), BF16),
            pltpu.VMEM((NC, SLAB + 2 * ROWS, HEADS * ROWS), BF16),
            pltpu.VMEM((NC, SLAB + 2 * ROWS, HEADS * ROWS), BF16),
            pltpu.VMEM((NC, ROWS, D), BF16),
            pltpu.VMEM((NC, ROWS, D), BF16),
            pltpu.VMEM((NP, ROWS, D), BF16),
            pltpu.VMEM((NP, ROWS, D), BF16),
            pltpu.VMEM((NC, ROWS, D), BF16),
            pltpu.VMEM((NC, ROWS, D), BF16),
            pltpu.VMEM((NC, HEADS, 256), F32),
            pltpu.VMEM((NC, HEADS, 256), F32),
            pltpu.VMEM((2, NP, 16, D), BF16),
            pltpu.VMEM((2, NP, 16, D), BF16),
            pltpu.VMEM((NP, HEADS, 128), F32),
            pltpu.VMEM((NP, HEADS, 128), F32),
            pltpu.VMEM((SLAB, D), F32),
            pltpu.VMEM((NP * 32, D), F32),
            pltpu.VMEM((NC * HEADS * ROWS, D), BF16),
            pltpu.SemaphoreType.DMA((6,)),
            pltpu.SemaphoreType.DMA((11,)),
            pltpu.SemaphoreType.DMA((11,)),
        ],
        compiler_params=pltpu.CompilerParams(
            collective_id=0, has_side_effects=True, vmem_limit_bytes=56 * 1024 * 1024
        ),
    )(
        log_scale.reshape(1, 1),
        bias.reshape(1, 1),
        probe,
        text,
        patches.reshape(ROWS * PATCH, D),
        key_value_matrix,
        output_weight,
        text_weight,
        jnp.asarray(column_order()),
    )
    return pl.pallas_call(
        part_sums,
        out_shape=(
            jax.ShapeDtypeStruct((OWN, 2 * D), F32),
            jax.ShapeDtypeStruct((OWN, D), F32),
            jax.ShapeDtypeStruct((OWN, D), F32),
            jax.ShapeDtypeStruct((D,), F32),
            jax.ShapeDtypeStruct((ROWS, D), BF16),
        ),
        in_specs=[vmem] * 2,
        out_specs=(vmem,) * 5,
    )(*sums)


def solution(mesh):
    rows = P(("loop", "grp"), None)
    return jax.shard_map(
        shards,
        mesh=mesh,
        in_specs=(P(("loop", "grp"), None, None), P(), P(), P(), rows, P(), P(), P()),
        out_specs=(rows, rows, rows, P(), rows),
        check_vma=False,
    )
```

```python
import functools
import math

import jax
import jax.numpy as jnp
import ml_dtypes
import numpy as np
from jax import lax
from jax.experimental import pallas as pl
from jax.experimental.pallas import tpu as pltpu
from jax.sharding import PartitionSpec as P

HEADS = 16
D = 1152
HEAD = D // HEADS
PATCH = 32
ROWS = 16
NC = 8
NP = 16
SLAB = D // NC
OWN = SLAB // NP
SPARE = SLAB - 128
ROOT = math.sqrt(HEAD)
MESH = pl.DeviceIdType.MESH
F32 = jnp.float32
BF16 = jnp.bfloat16


def nn(a, b):
    return lax.dot_general(a, b, (((1,), (0,)), ((), ())), preferred_element_type=F32)


def nt(a, b):
    return lax.dot_general(a, b, (((1,), (1,)), ((), ())), preferred_element_type=F32)


def flip(a):
    return a.astype(F32).T.astype(BF16)


def exact(a, b):
    return lax.dot_general(
        a,
        b,
        (((1,), (0,)), ((), ())),
        preferred_element_type=F32,
        precision=lax.Precision.HIGHEST,
    )


def iota(shape, dim):
    return lax.broadcasted_iota(jnp.int32, shape, dim)


def slab_of(values, start):
    block, shift = divmod(start, 128)
    first = values[:, 128 * block : 128 * block + 128]
    if shift == 0:
        return first
    first = pltpu.roll(first, 128 - shift, 1)
    if 128 * block + 128 >= values.shape[1]:
        return first
    second = pltpu.roll(values[:, 128 * block + 128 : 128 * block + 256], 128 - shift, 1)
    return jnp.where(iota(first.shape, 1) < 128 - shift, first, second)


def send_all(peer_of, count, me, source, target, send_sem, recv_sem):
    for step in range(1, count):
        peer = (me + step) & (count - 1)
        pltpu.make_async_remote_copy(
            src_ref=source(peer),
            dst_ref=target(me),
            send_sem=send_sem,
            recv_sem=recv_sem,
            device_id=peer_of(peer),
            device_id_type=MESH,
        ).start()


def all_but_one(peer_of, count, me, target, send_sem, recv_sem):
    part = target(pl.ds(0, count - 1))
    return pltpu.make_async_remote_copy(
        src_ref=part,
        dst_ref=part,
        send_sem=send_sem,
        recv_sem=recv_sem,
        device_id=peer_of(lax.rem(me + 1, count)),
        device_id_type=MESH,
    )


def slot_sum(ref, count):
    total = ref[0].astype(F32)
    for slot in range(1, count):
        total = total + ref[slot].astype(F32)
    return total


def unit_backward(gradient, unit, length):
    return (gradient - unit * jnp.sum(unit * gradient, axis=1, keepdims=True)) / length


def kernel(
    scale_ref,
    bias_ref,
    probe_ref,
    text_ref,
    x_hbm,
    wkv_hbm,
    wout_hbm,
    wtext_hbm,
    order_hbm,
    sums_ref,
    gfeat_ref,
    x_ref,
    wk_ref,
    keys_ref,
    values_ref,
    sorted_ref,
    wv_ref,
    wout_ref,
    wtext_ref,
    order_ref,
    mask_ref,
    soft_ref,
    texts,
    images,
    slab_out,
    slab_in,
    iret_out,
    iret_in,
    tret_out,
    tret_in,
    tgo_all,
    igo_all,
    small_out,
    small_in,
    last_out,
    last_in,
    tiny_out,
    tiny_in,
    part_ref,
    last_f32,
    heads_ref,
    load_sem,
    send_sem,
    recv_sem,
    share_sem,
):
    l = lax.axis_index("loop")
    k = lax.axis_index("grp")
    c = (l & 1) * 4 + (k & 1) * 2 + ((l >> 1) & 1)
    s = (l & 12) + (k >> 1)

    def in_column(peer):
        return {
            "loop": (l & 12) + (peer & 1) * 2 + (peer >> 2),
            "grp": (k & 6) + ((peer >> 1) & 1),
        }

    def in_plane(peer):
        return {"loop": (peer & 12) + (l & 3), "grp": (peer & 3) * 2 + (k & 1)}

    barrier = pltpu.get_barrier_semaphore()
    for peer_of, count, me in ((in_plane, NP, s), (in_column, NC, c)):
        for step in range(1, count):
            pl.semaphore_signal(
                barrier,
                inc=1,
                device_id=peer_of((me + step) & (count - 1)),
                device_id_type=MESH,
            )

    def load(source, target, number):
        return pltpu.make_async_copy(source, target, load_sem.at[number])

    loads = [
        load(wtext_hbm, wtext_ref, 0),
        load(wkv_hbm.at[:, :D], wk_ref, 1),
        load(x_hbm, x_ref, 2),
        load(wkv_hbm.at[:, D:], wv_ref, 3),
        load(wout_hbm, wout_ref, 4),
        load(order_hbm, order_ref, 5),
    ]
    for number in range(3):
        loads[number].start()

    column = (in_column, NC, c)
    plane = (in_plane, NP, s)
    phases = {
        0: (plane, lambda i: texts.at[i]),
        1: (column, lambda i: images.at[i]),
        2: (plane, lambda i: tret_in.at[i]),
        3: (column, lambda i: iret_in.at[i]),
        4: (column, lambda i: slab_in.at[i]),
        5: (column, lambda i: igo_all.at[i]),
        6: (column, lambda i: tgo_all.at[i]),
        7: (column, lambda i: small_in.at[i]),
        8: (plane, lambda i: last_in.at[0, i]),
        9: (plane, lambda i: last_in.at[1, i]),
        10: (plane, lambda i: tiny_in.at[i]),
    }
    started = []

    def copies(phase):
        (peer_of, count, me), target = phases[phase]
        return all_but_one(peer_of, count, me, target, send_sem.at[phase], recv_sem.at[phase])

    def send(phase, source):
        (peer_of, count, me), target = phases[phase]
        send_all(peer_of, count, me, source, target, send_sem.at[phase], recv_sem.at[phase])
        started.append(phase)

    def block_copy(phase, slots, peer, number):
        block = phases[phase][1](slots)
        return pltpu.make_async_remote_copy(
            src_ref=block,
            dst_ref=block,
            send_sem=send_sem.at[phase],
            recv_sem=share_sem.at[phase, number],
            device_id=in_column(peer),
            device_id_type=MESH,
        )

    def share(phase):
        for step in (2, 1, 3):
            block_copy(phase, c, (c & 4) + ((c + step) & 3), step).start()
        block_copy(phase, c, c ^ 4, 0).start()
        started.append(phase)

    def arrive_shared(phase):
        for step in (1, 3, 2):
            slot = (c & 4) + ((c - step) & 3)
            block_copy(phase, slot, c ^ 4, step).wait_recv()
            block_copy(phase, slot, c ^ 4, 0).start()
        block_copy(phase, pl.ds((c & 4) ^ 4, 4), c ^ 4, 0).wait_recv()

    def arrive(phase):
        copies(phase).wait_recv()

    head_of_row = iota((HEADS * ROWS, D), 0) >> 4
    lane = iota((HEADS * ROWS, D), 1)
    in_head = (lane >= head_of_row * HEAD) & (lane < head_of_row * HEAD + HEAD)
    mask_ref[...] = jnp.where(in_head, 1.0, 0.0).astype(BF16)

    loads[0].wait()
    loads[3].start()
    text_out = nn(text_ref[...], wtext_ref[...])
    text_length = jnp.sqrt(jnp.sum(text_out * text_out, axis=1, keepdims=True) + 1e-06)
    text_unit = text_out / text_length
    texts[s] = text_unit.astype(BF16)

    query = probe_ref[...].reshape(1, D).astype(BF16).astype(F32)
    query_heads = (mask_ref[...].astype(F32) * query).astype(BF16)
    loads[1].wait()
    loads[2].wait()
    loads[4].start()
    loads[5].start()
    for block in range(3):
        columns = slice(384 * block, 384 * block + 384)
        keys_ref[:, columns] = nn(x_ref[...], wk_ref[:, columns]).astype(BF16)
    scores = nt(keys_ref[...], query_heads) / ROOT

    same = (iota((ROWS * PATCH, HEADS * ROWS), 0) >> 5) == (
        iota((ROWS * PATCH, HEADS * ROWS), 1) & (ROWS - 1)
    )
    highest = jnp.max(jnp.where(same, scores, -jnp.inf), axis=0, keepdims=True)
    powers = jnp.where(same, jnp.exp(scores - highest), 0.0)
    weights = powers / jnp.sum(powers, axis=0, keepdims=True)
    soft_ref[...] = weights
    pl.semaphore_wait(barrier, NP + NC - 2)
    send(0, lambda p: texts.at[s])

    weights_t = weights.T.astype(BF16)

    patch_sums = nn(weights_t, x_ref[...]).astype(BF16)
    loads[3].wait()
    mixed = nn(patch_sums, wv_ref[...]) * mask_ref[...].astype(F32)
    pooled = jnp.sum(mixed.reshape(HEADS, ROWS, D), axis=0)
    pooled_half = pooled.astype(BF16)
    loads[4].wait()
    image_out = nn(pooled_half, wout_ref[...])
    image_length = jnp.sqrt(jnp.sum(image_out * image_out, axis=1, keepdims=True) + 1e-06)
    image_unit = image_out / image_length
    images[c] = image_unit.astype(BF16)
    share(1)

    features = jnp.concatenate([pooled_half, text_ref[...]], axis=0)
    loads[5].wait()
    slab_out[:, :SLAB, :] = nt(order_ref[...], patch_sums).astype(BF16).reshape(
        NC, SLAB, HEADS * ROWS
    )
    for place in range(NC):
        rows = order_ref[SLAB * place : SLAB * place + SLAB, :]
        slab_out[place, SLAB:, :SLAB] = nt(features, rows).astype(BF16)
    slab_in[c] = slab_out[c]
    send(4, lambda p: slab_out.at[p])

    temperature = jnp.exp(scale_ref[...])
    arrive(0)
    arrive_shared(1)
    text_all = texts[...].reshape(NP * ROWS, D)
    image_all = images[...].reshape(NC * ROWS, D)
    logits = temperature * nt(image_all, text_all) + bias_ref[...]
    row = iota((NC * ROWS, NP * ROWS), 0)
    col = iota((NC * ROWS, NP * ROWS), 1)
    matched = ((row >> 4) == c) & ((col >> 4) == s) & ((row & 15) == (col & 15))
    sign = jnp.where(matched, 1.0, -1.0)
    coeff = -sign / (1.0 + jnp.exp(sign * logits))
    iret_out[...] = nn(coeff.astype(BF16), text_all).astype(BF16).reshape(NC, ROWS, D)
    iret_in[c] = iret_out[c]
    send(3, lambda p: iret_out.at[p])
    tret_out[...] = nn(flip(coeff), image_all).astype(BF16).reshape(NP, ROWS, D)
    tret_in[s] = tret_out[s]
    send(2, lambda p: tret_out.at[p])

    for block in range(3):
        columns = slice(384 * block, 384 * block + 384)
        values_ref[:, columns] = nn(x_ref[...], wv_ref[:, columns]).astype(BF16)
        sorted_ref[:, columns] = nt(x_ref[...], order_ref[columns, :]).astype(BF16)

    arrive(3)
    image_returned = temperature * slot_sum(iret_in, NC)
    image_grad = unit_backward(image_returned, image_unit, image_length).astype(BF16)
    igo_all[c] = image_grad
    share(5)

    pooled_grad = nt(image_grad, wout_ref[...]).astype(BF16).astype(F32)
    tiled = jnp.concatenate([pooled_grad] * HEADS, axis=0)
    grad_heads = (mask_ref[...].astype(F32) * tiled).astype(BF16)
    weight_grad = nt(values_ref[...], grad_heads)
    weights = soft_ref[...]
    inner = jnp.sum(weights * weight_grad, axis=0, keepdims=True)
    score_grad = (weights * (weight_grad - inner)).astype(BF16)
    fold = jnp.where((iota((HEADS * ROWS, 128), 0) >> 4) == iota((HEADS * ROWS, 128), 1), 1.0, 0.0)
    score_grad_t = nn(score_grad, fold.astype(BF16)).T[:HEADS].astype(BF16)

    arrive(2)
    text_returned = temperature * slot_sum(tret_in, NP)
    text_grad = unit_backward(text_returned, text_unit, text_length).astype(BF16)
    tgo_all[c] = text_grad
    share(6)

    key_sum = nn(score_grad_t, sorted_ref[...])
    head_row = iota((HEADS, D), 0)
    head_col = iota((HEADS, D), 1)
    own_head = (head_col >= head_row * HEAD) & (head_col < head_row * HEAD + HEAD)
    probe_sum = jnp.where(own_head, nn(score_grad_t, keys_ref[...]), 0.0) / ROOT
    tile_row = iota((HEADS, 128), 0)
    tile_lane = iota((HEADS, 128), 1)
    probe_tile = jnp.zeros((HEADS, 128), F32)
    for head in range(HEADS):
        probe_tile = jnp.where(tile_row == head, slab_of(probe_sum, HEAD * head), probe_tile)
    probe_tile = pltpu.roll(probe_tile, SPARE, 1)
    for place in range(NC):
        start = SLAB * place
        small_out[place, :, :128] = slab_of(key_sum, start)
        small_out[place, :, 128:] = jnp.where(
            tile_lane < SPARE, slab_of(key_sum, start + 128), probe_tile
        )
    small_in[c] = small_out[c]
    send(7, lambda p: small_out.at[p])

    last_f32[...] = jnp.zeros_like(last_f32)

    def place_rows(offset):
        for part in range(NP):
            last_f32[32 * part + offset : 32 * part + offset + OWN, :] = part_ref[
                OWN * part : OWN * part + OWN, :
            ]

    arrive(4)
    arrive_shared(5)
    igo = igo_all[...].reshape(NC * ROWS, D)
    part_ref[...] = nn(flip(slab_in[:, SLAB : SLAB + ROWS, :].reshape(NC * ROWS, 256))[:SLAB], igo)
    place_rows(0)
    pooled_grads = nt(igo, wout_ref[...]).astype(BF16)
    for place in range(NC):
        tiled = jnp.concatenate([pooled_grads[ROWS * place : ROWS * place + ROWS]] * HEADS, axis=0)
        heads_ref[256 * place : 256 * place + 256, :] = mask_ref[...] * tiled
    left = jnp.concatenate([slab_in[place, :SLAB, :] for place in range(NC)], axis=1)
    part_ref[...] = nn(left, heads_ref[...])
    place_rows(OWN)

    def pack(half):
        rows = last_f32[...].reshape(NP, 32, D)[:, 16 * half : 16 * half + 16]
        last_out[half] = rows.astype(BF16)
        last_in[half, s] = last_out[half, s]

    pack(0)
    send(8, lambda p: last_out.at[0, p])

    arrive(7)
    tiny = slot_sum(small_in, NC)
    for place in range(NP):
        tiny_out[place] = jnp.where(
            tile_lane < SPARE, slab_of(tiny, OWN * place), tiny[:, 128:]
        )
    tiny_in[s] = tiny_out[s]
    send(10, lambda p: tiny_out.at[p])

    arrive_shared(6)
    tgo = tgo_all[...].reshape(NC * ROWS, D)
    part_ref[...] = nn(flip(slab_in[:, SLAB + ROWS :, :].reshape(NC * ROWS, 256))[:SLAB], tgo)
    place_rows(2 * OWN)
    pack(1)
    send(9, lambda p: last_out.at[1, p])

    gfeat_ref[...] = nt(text_grad, wtext_ref[...]).astype(BF16)

    arrive(10)
    tiny = slot_sum(tiny_in, NP)
    probe_tile = pltpu.roll(tiny, 128 - SPARE, 1)
    spread = jnp.where(iota((128, D), 0) == iota((1, D), 1) % HEAD, 1.0, 0.0)
    probe_grad = exact(probe_tile, spread)
    sums_ref[48:56, :] = jnp.broadcast_to(
        jnp.sum(jnp.where(own_head, probe_grad, 0.0), axis=0, keepdims=True), (8, D)
    )
    sums_ref[32:48, :] = exact(tiny.T[:16, :], jnp.where(own_head, query, 0.0) / ROOT)

    arrive(8)
    sums_ref[:16, :] = slot_sum(last_in.at[0], NP)
    arrive(9)
    sums_ref[16:32, :] = slot_sum(last_in.at[1], NP)

    for phase in started:
        copies(phase).wait_send()


def part_sums(sums_ref, feat_ref, gkv_ref, gout_ref, gtext_ref, gprobe_ref, gfeat_ref):
    gout_ref[...] = sums_ref[:OWN, :]
    gkv_ref[:, :D] = sums_ref[32 : 32 + OWN, :]
    gkv_ref[:, D:] = sums_ref[OWN : 2 * OWN, :]
    gtext_ref[...] = sums_ref[2 * OWN : 3 * OWN, :]
    gprobe_ref[...] = sums_ref[48:49, :].reshape(D)
    gfeat_ref[...] = feat_ref[...]


def column_order():
    c, s, r = np.meshgrid(np.arange(NC), np.arange(NP), np.arange(OWN), indexing="ij")
    loop = (s // 4) * 4 + (c % 2) * 2 + c // 4
    grp = (s % 4) * 2 + c // 2 % 2
    kept = ((loop * 8 + grp) * OWN + r).reshape(D)
    return (kept[:, None] == np.arange(D)[None, :]).astype(ml_dtypes.bfloat16)


def shards(patches, probe, key_value_matrix, output_weight, text, text_weight, log_scale, bias):
    vmem = pl.BlockSpec(memory_space=pltpu.VMEM)
    anywhere = pl.BlockSpec(memory_space=pl.ANY)
    sums = pl.pallas_call(
        kernel,
        out_shape=(
            jax.ShapeDtypeStruct((56, D), F32),
            jax.ShapeDtypeStruct((ROWS, D), BF16),
        ),
        in_specs=[vmem] * 4 + [anywhere] * 5,
        out_specs=(vmem,) * 2,
        scratch_shapes=[
            pltpu.VMEM((ROWS * PATCH, D), BF16),
            pltpu.VMEM((D, D), BF16),
            pltpu.VMEM((ROWS * PATCH, D), BF16),
            pltpu.VMEM((ROWS * PATCH, D), BF16),
            pltpu.VMEM((ROWS * PATCH, D), BF16),
            pltpu.VMEM((D, D), BF16),
            pltpu.VMEM((D, D), BF16),
            pltpu.VMEM((D, D), BF16),
            pltpu.VMEM((D, D), BF16),
            pltpu.VMEM((HEADS * ROWS, D), BF16),
            pltpu.VMEM((ROWS * PATCH, HEADS * ROWS), F32),
            pltpu.VMEM((NP, ROWS, D), BF16),
            pltpu.VMEM((NC, ROWS, D), BF16),
            pltpu.VMEM((NC, SLAB + 2 * ROWS, HEADS * ROWS), BF16),
            pltpu.VMEM((NC, SLAB + 2 * ROWS, HEADS * ROWS), BF16),
            pltpu.VMEM((NC, ROWS, D), BF16),
            pltpu.VMEM((NC, ROWS, D), BF16),
            pltpu.VMEM((NP, ROWS, D), BF16),
            pltpu.VMEM((NP, ROWS, D), BF16),
            pltpu.VMEM((NC, ROWS, D), BF16),
            pltpu.VMEM((NC, ROWS, D), BF16),
            pltpu.VMEM((NC, HEADS, 256), F32),
            pltpu.VMEM((NC, HEADS, 256), F32),
            pltpu.VMEM((2, NP, 16, D), BF16),
            pltpu.VMEM((2, NP, 16, D), BF16),
            pltpu.VMEM((NP, HEADS, 128), F32),
            pltpu.VMEM((NP, HEADS, 128), F32),
            pltpu.VMEM((SLAB, D), F32),
            pltpu.VMEM((NP * 32, D), F32),
            pltpu.VMEM((NC * HEADS * ROWS, D), BF16),
            pltpu.SemaphoreType.DMA((6,)),
            pltpu.SemaphoreType.DMA((11,)),
            pltpu.SemaphoreType.DMA((11,)),
            pltpu.SemaphoreType.DMA((11, 4)),
        ],
        compiler_params=pltpu.CompilerParams(
            collective_id=0, has_side_effects=True, vmem_limit_bytes=56 * 1024 * 1024
        ),
    )(
        log_scale.reshape(1, 1),
        bias.reshape(1, 1),
        probe,
        text,
        patches.reshape(ROWS * PATCH, D),
        key_value_matrix,
        output_weight,
        text_weight,
        jnp.asarray(column_order()),
    )
    return pl.pallas_call(
        part_sums,
        out_shape=(
            jax.ShapeDtypeStruct((OWN, 2 * D), F32),
            jax.ShapeDtypeStruct((OWN, D), F32),
            jax.ShapeDtypeStruct((OWN, D), F32),
            jax.ShapeDtypeStruct((D,), F32),
            jax.ShapeDtypeStruct((ROWS, D), BF16),
        ),
        in_specs=[vmem] * 2,
        out_specs=(vmem,) * 5,
    )(*sums)


def solution(mesh):
    rows = P(("loop", "grp"), None)
    return jax.shard_map(
        shards,
        mesh=mesh,
        in_specs=(P(("loop", "grp"), None, None), P(), P(), P(), rows, P(), P(), P()),
        out_specs=(rows, rows, rows, P(), rows),
        check_vma=False,
    )
```

```python
import functools
import math

import jax
import jax.numpy as jnp
import ml_dtypes
import numpy as np
from jax import lax
from jax.experimental import pallas as pl
from jax.experimental.pallas import tpu as pltpu
from jax.sharding import PartitionSpec as P

HEADS = 16
D = 1152
HEAD = D // HEADS
PATCH = 32
ROWS = 16
NC = 8
NP = 16
SLAB = D // NC
OWN = SLAB // NP
SPARE = SLAB - 128
ROOT = math.sqrt(HEAD)
MESH = pl.DeviceIdType.MESH
F32 = jnp.float32
BF16 = jnp.bfloat16


def nn(a, b):
    return lax.dot_general(a, b, (((1,), (0,)), ((), ())), preferred_element_type=F32)


def nt(a, b):
    return lax.dot_general(a, b, (((1,), (1,)), ((), ())), preferred_element_type=F32)


def flip(a):
    return a.astype(F32).T.astype(BF16)


def exact(a, b):
    return lax.dot_general(
        a,
        b,
        (((1,), (0,)), ((), ())),
        preferred_element_type=F32,
        precision=lax.Precision.HIGHEST,
    )


def iota(shape, dim):
    return lax.broadcasted_iota(jnp.int32, shape, dim)


def slab_of(values, start):
    block, shift = divmod(start, 128)
    first = values[:, 128 * block : 128 * block + 128]
    if shift == 0:
        return first
    first = pltpu.roll(first, 128 - shift, 1)
    if 128 * block + 128 >= values.shape[1]:
        return first
    second = pltpu.roll(values[:, 128 * block + 128 : 128 * block + 256], 128 - shift, 1)
    return jnp.where(iota(first.shape, 1) < 128 - shift, first, second)


def send_all(peer_of, count, me, source, target, send_sem, recv_sem):
    for step in range(1, count):
        peer = (me + step) & (count - 1)
        pltpu.make_async_remote_copy(
            src_ref=source(peer),
            dst_ref=target(me),
            send_sem=send_sem,
            recv_sem=recv_sem,
            device_id=peer_of(peer),
            device_id_type=MESH,
        ).start()


def all_but_one(peer_of, count, me, target, send_sem, recv_sem):
    part = target(pl.ds(0, count - 1))
    return pltpu.make_async_remote_copy(
        src_ref=part,
        dst_ref=part,
        send_sem=send_sem,
        recv_sem=recv_sem,
        device_id=peer_of(lax.rem(me + 1, count)),
        device_id_type=MESH,
    )


def slot_sum(ref, count):
    total = ref[0].astype(F32)
    for slot in range(1, count):
        total = total + ref[slot].astype(F32)
    return total


def unit_backward(gradient, unit, length):
    return (gradient - unit * jnp.sum(unit * gradient, axis=1, keepdims=True)) / length


def kernel(
    scale_ref,
    bias_ref,
    probe_ref,
    text_ref,
    x_hbm,
    wkv_hbm,
    wout_hbm,
    wtext_hbm,
    order_hbm,
    sums_ref,
    gfeat_ref,
    x_ref,
    wk_ref,
    keys_ref,
    values_ref,
    sorted_ref,
    wv_ref,
    wout_ref,
    wout_t_ref,
    wtext_ref,
    order_ref,
    mask_ref,
    soft_ref,
    texts,
    images,
    slab_out,
    slab_in,
    feat_out,
    feat_in,
    iret_out,
    iret_half,
    iret_sum,
    iret_in,
    tret_out,
    tret_in,
    tgo_all,
    igo_all,
    small_out,
    small_in,
    last_out,
    last_in,
    tiny_out,
    tiny_in,
    part_ref,
    last_f32,
    heads_ref,
    load_sem,
    send_sem,
    recv_sem,
    share_sem,
    quarter_sem,
):
    l = lax.axis_index("loop")
    k = lax.axis_index("grp")
    c = (l & 1) * 4 + (k & 1) * 2 + ((l >> 1) & 1)
    s = (l & 12) + (k >> 1)

    def in_column(peer):
        return {
            "loop": (l & 12) + (peer & 1) * 2 + (peer >> 2),
            "grp": (k & 6) + ((peer >> 1) & 1),
        }

    def in_plane(peer):
        return {"loop": (peer & 12) + (l & 3), "grp": (peer & 3) * 2 + (k & 1)}

    barrier = pltpu.get_barrier_semaphore()
    for peer_of, count, me in ((in_plane, NP, s), (in_column, NC, c)):
        for step in range(1, count):
            pl.semaphore_signal(
                barrier,
                inc=1,
                device_id=peer_of((me + step) & (count - 1)),
                device_id_type=MESH,
            )

    def load(source, target, number):
        return pltpu.make_async_copy(source, target, load_sem.at[number])

    loads = [
        load(wtext_hbm, wtext_ref, 0),
        load(wkv_hbm.at[:, :D], wk_ref, 1),
        load(x_hbm, x_ref, 2),
        load(wkv_hbm.at[:, D:], wv_ref, 3),
        load(wout_hbm, wout_ref, 4),
        load(order_hbm, order_ref, 5),
    ]
    for number in range(3):
        loads[number].start()

    column = (in_column, NC, c)
    plane = (in_plane, NP, s)
    phases = {
        0: (plane, lambda i: texts.at[i]),
        1: (column, lambda i: images.at[i]),
        2: (plane, lambda i: tret_in.at[i]),
        4: (column, lambda i: slab_in.at[i]),
        5: (column, lambda i: igo_all.at[i]),
        6: (column, lambda i: tgo_all.at[i]),
        7: (column, lambda i: small_in.at[i]),
        8: (plane, lambda i: last_in.at[0, i]),
        9: (plane, lambda i: last_in.at[1, i]),
        10: (plane, lambda i: tiny_in.at[i]),
        11: (column, lambda i: feat_in.at[i]),
    }
    started = []

    def copies(phase):
        (peer_of, count, me), target = phases[phase]
        return all_but_one(peer_of, count, me, target, send_sem.at[phase], recv_sem.at[phase])

    def send(phase, source):
        (peer_of, count, me), target = phases[phase]
        send_all(peer_of, count, me, source, target, send_sem.at[phase], recv_sem.at[phase])
        started.append(phase)

    def block_copy(phase, slots, peer, number):
        block = phases[phase][1](slots)
        return pltpu.make_async_remote_copy(
            src_ref=block,
            dst_ref=block,
            send_sem=send_sem.at[phase],
            recv_sem=share_sem.at[phase, number],
            device_id=in_column(peer),
            device_id_type=MESH,
        )

    def share(phase):
        for step in (2, 1, 3):
            block_copy(phase, c, (c & 4) + ((c + step) & 3), step).start()
        block_copy(phase, c, c ^ 4, 0).start()
        started.append(phase)

    def arrive_shared(phase):
        for step in (1, 3, 2):
            slot = (c & 4) + ((c - step) & 3)
            block_copy(phase, slot, c ^ 4, step).wait_recv()
            block_copy(phase, slot, c ^ 4, 0).start()
        block_copy(phase, pl.ds((c & 4) ^ 4, 4), c ^ 4, 0).wait_recv()

    def arrive(phase):
        copies(phase).wait_recv()

    head_of_row = iota((HEADS * ROWS, D), 0) >> 4
    lane = iota((HEADS * ROWS, D), 1)
    in_head = (lane >= head_of_row * HEAD) & (lane < head_of_row * HEAD + HEAD)
    mask_ref[...] = jnp.where(in_head, 1.0, 0.0).astype(BF16)

    loads[0].wait()
    loads[3].start()
    text_out = nn(text_ref[...], wtext_ref[...])
    text_length = jnp.sqrt(jnp.sum(text_out * text_out, axis=1, keepdims=True) + 1e-06)
    text_unit = text_out / text_length
    texts[s] = text_unit.astype(BF16)

    query = probe_ref[...].reshape(1, D).astype(BF16).astype(F32)
    query_heads = (mask_ref[...].astype(F32) * query).astype(BF16)
    loads[1].wait()
    loads[2].wait()
    loads[4].start()
    loads[5].start()
    for block in range(3):
        columns = slice(384 * block, 384 * block + 384)
        keys_ref[:, columns] = nn(x_ref[...], wk_ref[:, columns]).astype(BF16)
        if block == 1:
            pl.semaphore_wait(barrier, NP + NC - 2)
            send(0, lambda p: texts.at[s])
    scores = nt(keys_ref[...], query_heads) / ROOT

    same = (iota((ROWS * PATCH, HEADS * ROWS), 0) >> 5) == (
        iota((ROWS * PATCH, HEADS * ROWS), 1) & (ROWS - 1)
    )
    highest = jnp.max(jnp.where(same, scores, -jnp.inf), axis=0, keepdims=True)
    powers = jnp.where(same, jnp.exp(scores - highest), 0.0)
    weights = powers / jnp.sum(powers, axis=0, keepdims=True)
    soft_ref[...] = weights
    weights_t = weights.T.astype(BF16)

    patch_sums = nn(weights_t, x_ref[...]).astype(BF16)
    loads[3].wait()
    mixed = nn(patch_sums, wv_ref[...]) * mask_ref[...].astype(F32)
    pooled = jnp.sum(mixed.reshape(HEADS, ROWS, D), axis=0)
    pooled_half = pooled.astype(BF16)
    loads[4].wait()
    image_out = nn(pooled_half, wout_ref[...])
    image_length = jnp.sqrt(jnp.sum(image_out * image_out, axis=1, keepdims=True) + 1e-06)
    image_unit = image_out / image_length
    images[c] = image_unit.astype(BF16)
    share(1)

    loads[5].wait()
    slab_out[...] = nt(order_ref[...], patch_sums).astype(BF16).reshape(NC, SLAB, HEADS * ROWS)
    slab_in[c] = slab_out[c]
    send(4, lambda p: slab_out.at[p])
    features = jnp.concatenate([pooled_half, text_ref[...]], axis=0)
    for place in range(NC):
        rows = order_ref[SLAB * place : SLAB * place + SLAB, :]
        feat_out[place, :, :SLAB] = nt(features, rows).astype(BF16)
    feat_in[c] = feat_out[c]
    send(11, lambda p: feat_out.at[p])

    for block in range(3):
        rows = slice(384 * block, 384 * block + 384)
        wout_t_ref[:, rows] = flip(wout_ref[rows, :])

    temperature = jnp.exp(scale_ref[...])
    arrive(0)
    arrive_shared(1)
    text_all = texts[...].reshape(NP * ROWS, D)
    image_all = images[...].reshape(NC * ROWS, D)
    logits = temperature * nt(image_all, text_all) + bias_ref[...]
    row = iota((NC * ROWS, NP * ROWS), 0)
    col = iota((NC * ROWS, NP * ROWS), 1)
    matched = ((row >> 4) == c) & ((col >> 4) == s) & ((row & 15) == (col & 15))
    sign = jnp.where(matched, 1.0, -1.0)
    coeff = -sign / (1.0 + jnp.exp(sign * logits))
    iret_out[...] = nn(coeff.astype(BF16), text_all).astype(BF16).reshape(NC, ROWS, D)
    halves = pltpu.make_async_remote_copy(
        src_ref=iret_out.at[pl.ds((c & 4) ^ 4, 4)],
        dst_ref=iret_half,
        send_sem=send_sem.at[3],
        recv_sem=recv_sem.at[3],
        device_id=in_column(c ^ 4),
        device_id_type=MESH,
    )
    halves.start()
    tret_out[...] = nn(flip(coeff), image_all).astype(BF16).reshape(NP, ROWS, D)
    tret_in[s] = tret_out[s]
    send(2, lambda p: tret_out.at[p])
    halves.wait_recv()
    iret_sum[...] = (
        iret_out[pl.ds(c & 4, 4)].astype(F32) + iret_half[...].astype(F32)
    ).astype(BF16)
    iret_in[c & 3] = iret_sum[c & 3]

    def quarter(step, slot):
        return pltpu.make_async_remote_copy(
            src_ref=iret_sum.at[slot],
            dst_ref=iret_in.at[c & 3],
            send_sem=quarter_sem.at[0, step],
            recv_sem=quarter_sem.at[1, step],
            device_id=in_column((c & 4) + slot),
            device_id_type=MESH,
        )

    quarters = [quarter(step, (c + step) & 3) for step in (2, 1, 3)]
    for copy in quarters:
        copy.start()

    for block in range(3):
        columns = slice(384 * block, 384 * block + 384)
        values_ref[:, columns] = nn(x_ref[...], wv_ref[:, columns]).astype(BF16)
        sorted_ref[:, columns] = nt(x_ref[...], order_ref[columns, :]).astype(BF16)
    last_f32[...] = jnp.zeros_like(last_f32)

    for copy in quarters:
        copy.wait_recv()
    image_returned = temperature * slot_sum(iret_in, 4)
    image_grad = unit_backward(image_returned, image_unit, image_length).astype(BF16)
    igo_all[c] = image_grad
    share(5)

    pooled_grad = nn(image_grad, wout_t_ref[...]).astype(BF16).astype(F32)
    tiled = jnp.concatenate([pooled_grad] * HEADS, axis=0)
    grad_heads = (mask_ref[...].astype(F32) * tiled).astype(BF16)
    weight_grad = nt(values_ref[...], grad_heads)
    weights = soft_ref[...]
    inner = jnp.sum(weights * weight_grad, axis=0, keepdims=True)
    score_grad = (weights * (weight_grad - inner)).astype(BF16)
    fold = jnp.where((iota((HEADS * ROWS, 128), 0) >> 4) == iota((HEADS * ROWS, 128), 1), 1.0, 0.0)
    score_grad_t = nn(score_grad, fold.astype(BF16)).T[:HEADS].astype(BF16)

    arrive(2)
    text_returned = temperature * slot_sum(tret_in, NP)
    text_grad = unit_backward(text_returned, text_unit, text_length).astype(BF16)
    tgo_all[c] = text_grad
    share(6)

    key_sum = nn(score_grad_t, sorted_ref[...])
    head_row = iota((HEADS, D), 0)
    head_col = iota((HEADS, D), 1)
    own_head = (head_col >= head_row * HEAD) & (head_col < head_row * HEAD + HEAD)
    probe_sum = jnp.where(own_head, nn(score_grad_t, keys_ref[...]), 0.0) / ROOT
    tile_row = iota((HEADS, 128), 0)
    tile_lane = iota((HEADS, 128), 1)
    probe_tile = jnp.zeros((HEADS, 128), F32)
    for head in range(HEADS):
        probe_tile = jnp.where(tile_row == head, slab_of(probe_sum, HEAD * head), probe_tile)
    probe_tile = pltpu.roll(probe_tile, SPARE, 1)
    for place in range(NC):
        start = SLAB * place
        small_out[place, :, :128] = slab_of(key_sum, start)
        small_out[place, :, 128:] = jnp.where(
            tile_lane < SPARE, slab_of(key_sum, start + 128), probe_tile
        )
    small_in[c] = small_out[c]
    send(7, lambda p: small_out.at[p])


    def place_rows(offset):
        for part in range(NP):
            last_f32[32 * part + offset : 32 * part + offset + OWN, :] = part_ref[
                OWN * part : OWN * part + OWN, :
            ]

    arrive(11)
    arrive_shared(5)
    igo = igo_all[...].reshape(NC * ROWS, D)
    part_ref[...] = nn(flip(feat_in[:, :ROWS, :].reshape(NC * ROWS, 256))[:SLAB], igo)
    place_rows(0)
    pooled_grads = nn(igo, wout_t_ref[...]).astype(BF16)
    for place in range(NC):
        tiled = jnp.concatenate([pooled_grads[ROWS * place : ROWS * place + ROWS]] * HEADS, axis=0)
        heads_ref[256 * place : 256 * place + 256, :] = mask_ref[...] * tiled
    arrive(4)
    left = jnp.concatenate([slab_in[place] for place in range(NC)], axis=1)
    part_ref[...] = nn(left, heads_ref[...])
    place_rows(OWN)

    def pack(half):
        rows = last_f32[...].reshape(NP, 32, D)[:, 16 * half : 16 * half + 16]
        last_out[half] = rows.astype(BF16)
        last_in[half, s] = last_out[half, s]

    pack(0)
    send(8, lambda p: last_out.at[0, p])

    arrive_shared(6)
    tgo = tgo_all[...].reshape(NC * ROWS, D)
    part_ref[...] = nn(flip(feat_in[:, ROWS:, :].reshape(NC * ROWS, 256))[:SLAB], tgo)
    place_rows(2 * OWN)
    pack(1)
    arrive(7)
    tiny = slot_sum(small_in, NC)
    for place in range(NP):
        tiny_out[place] = jnp.where(
            tile_lane < SPARE, slab_of(tiny, OWN * place), tiny[:, 128:]
        )
    tiny_in[s] = tiny_out[s]
    send(10, lambda p: tiny_out.at[p])

    send(9, lambda p: last_out.at[1, p])

    gfeat_ref[...] = nt(text_grad, wtext_ref[...]).astype(BF16)

    arrive(10)
    tiny = slot_sum(tiny_in, NP)
    probe_tile = pltpu.roll(tiny, 128 - SPARE, 1)
    spread = jnp.where(iota((128, D), 0) == iota((1, D), 1) % HEAD, 1.0, 0.0)
    probe_grad = exact(probe_tile, spread)
    sums_ref[48:56, :] = jnp.broadcast_to(
        jnp.sum(jnp.where(own_head, probe_grad, 0.0), axis=0, keepdims=True), (8, D)
    )
    sums_ref[32:48, :] = exact(tiny.T[:16, :], jnp.where(own_head, query, 0.0) / ROOT)

    arrive(8)
    sums_ref[:16, :] = slot_sum(last_in.at[0], NP)
    arrive(9)
    sums_ref[16:32, :] = slot_sum(last_in.at[1], NP)

    for copy in [halves] + quarters:
        copy.wait_send()
    for phase in started:
        copies(phase).wait_send()


def part_sums(sums_ref, feat_ref, gkv_ref, gout_ref, gtext_ref, gprobe_ref, gfeat_ref):
    gout_ref[...] = sums_ref[:OWN, :]
    gkv_ref[:, :D] = sums_ref[32 : 32 + OWN, :]
    gkv_ref[:, D:] = sums_ref[OWN : 2 * OWN, :]
    gtext_ref[...] = sums_ref[2 * OWN : 3 * OWN, :]
    gprobe_ref[...] = sums_ref[48:49, :].reshape(D)
    gfeat_ref[...] = feat_ref[...]


def column_order():
    c, s, r = np.meshgrid(np.arange(NC), np.arange(NP), np.arange(OWN), indexing="ij")
    loop = (s // 4) * 4 + (c % 2) * 2 + c // 4
    grp = (s % 4) * 2 + c // 2 % 2
    kept = ((loop * 8 + grp) * OWN + r).reshape(D)
    return (kept[:, None] == np.arange(D)[None, :]).astype(ml_dtypes.bfloat16)


def shards(patches, probe, key_value_matrix, output_weight, text, text_weight, log_scale, bias):
    vmem = pl.BlockSpec(memory_space=pltpu.VMEM)
    anywhere = pl.BlockSpec(memory_space=pl.ANY)
    sums = pl.pallas_call(
        kernel,
        out_shape=(
            jax.ShapeDtypeStruct((56, D), F32),
            jax.ShapeDtypeStruct((ROWS, D), BF16),
        ),
        in_specs=[vmem] * 4 + [anywhere] * 5,
        out_specs=(vmem,) * 2,
        scratch_shapes=[
            pltpu.VMEM((ROWS * PATCH, D), BF16),
            pltpu.VMEM((D, D), BF16),
            pltpu.VMEM((ROWS * PATCH, D), BF16),
            pltpu.VMEM((ROWS * PATCH, D), BF16),
            pltpu.VMEM((ROWS * PATCH, D), BF16),
            pltpu.VMEM((D, D), BF16),
            pltpu.VMEM((D, D), BF16),
            pltpu.VMEM((D, D), BF16),
            pltpu.VMEM((D, D), BF16),
            pltpu.VMEM((D, D), BF16),
            pltpu.VMEM((HEADS * ROWS, D), BF16),
            pltpu.VMEM((ROWS * PATCH, HEADS * ROWS), F32),
            pltpu.VMEM((NP, ROWS, D), BF16),
            pltpu.VMEM((NC, ROWS, D), BF16),
            pltpu.VMEM((NC, SLAB, HEADS * ROWS), BF16),
            pltpu.VMEM((NC, SLAB, HEADS * ROWS), BF16),
            pltpu.VMEM((NC, 2 * ROWS, HEADS * ROWS), BF16),
            pltpu.VMEM((NC, 2 * ROWS, HEADS * ROWS), BF16),
            pltpu.VMEM((NC, ROWS, D), BF16),
            pltpu.VMEM((4, ROWS, D), BF16),
            pltpu.VMEM((4, ROWS, D), BF16),
            pltpu.VMEM((4, ROWS, D), BF16),
            pltpu.VMEM((NP, ROWS, D), BF16),
            pltpu.VMEM((NP, ROWS, D), BF16),
            pltpu.VMEM((NC, ROWS, D), BF16),
            pltpu.VMEM((NC, ROWS, D), BF16),
            pltpu.VMEM((NC, HEADS, 256), F32),
            pltpu.VMEM((NC, HEADS, 256), F32),
            pltpu.VMEM((2, NP, 16, D), BF16),
            pltpu.VMEM((2, NP, 16, D), BF16),
            pltpu.VMEM((NP, HEADS, 128), F32),
            pltpu.VMEM((NP, HEADS, 128), F32),
            pltpu.VMEM((SLAB, D), F32),
            pltpu.VMEM((NP * 32, D), F32),
            pltpu.VMEM((NC * HEADS * ROWS, D), BF16),
            pltpu.SemaphoreType.DMA((6,)),
            pltpu.SemaphoreType.DMA((12,)),
            pltpu.SemaphoreType.DMA((12,)),
            pltpu.SemaphoreType.DMA((11, 4)),
            pltpu.SemaphoreType.DMA((2, 4)),
        ],
        compiler_params=pltpu.CompilerParams(
            collective_id=0, has_side_effects=True, vmem_limit_bytes=56 * 1024 * 1024
        ),
    )(
        log_scale.reshape(1, 1),
        bias.reshape(1, 1),
        probe,
        text,
        patches.reshape(ROWS * PATCH, D),
        key_value_matrix,
        output_weight,
        text_weight,
        jnp.asarray(column_order()),
    )
    return pl.pallas_call(
        part_sums,
        out_shape=(
            jax.ShapeDtypeStruct((OWN, 2 * D), F32),
            jax.ShapeDtypeStruct((OWN, D), F32),
            jax.ShapeDtypeStruct((OWN, D), F32),
            jax.ShapeDtypeStruct((D,), F32),
            jax.ShapeDtypeStruct((ROWS, D), BF16),
        ),
        in_specs=[vmem] * 2,
        out_specs=(vmem,) * 5,
    )(*sums)


def solution(mesh):
    rows = P(("loop", "grp"), None)
    return jax.shard_map(
        shards,
        mesh=mesh,
        in_specs=(P(("loop", "grp"), None, None), P(), P(), P(), rows, P(), P(), P()),
        out_specs=(rows, rows, rows, P(), rows),
        check_vma=False,
    )
```

```python
import functools
import math

import jax
import jax.numpy as jnp
import ml_dtypes
import numpy as np
from jax import lax
from jax.experimental import pallas as pl
from jax.experimental.pallas import tpu as pltpu
from jax.sharding import PartitionSpec as P

HEADS = 16
D = 1152
HEAD = D // HEADS
PATCH = 32
ROWS = 16
NC = 8
NP = 16
SLAB = D // NC
OWN = SLAB // NP
SPARE = SLAB - 128
ROOT = math.sqrt(HEAD)
MESH = pl.DeviceIdType.MESH
F32 = jnp.float32
BF16 = jnp.bfloat16


def nn(a, b):
    return lax.dot_general(a, b, (((1,), (0,)), ((), ())), preferred_element_type=F32)


def nt(a, b):
    return lax.dot_general(a, b, (((1,), (1,)), ((), ())), preferred_element_type=F32)


def flip(a):
    return a.astype(F32).T.astype(BF16)


def exact(a, b):
    return lax.dot_general(
        a,
        b,
        (((1,), (0,)), ((), ())),
        preferred_element_type=F32,
        precision=lax.Precision.HIGHEST,
    )


def iota(shape, dim):
    return lax.broadcasted_iota(jnp.int32, shape, dim)


def slab_of(values, start):
    block, shift = divmod(start, 128)
    first = values[:, 128 * block : 128 * block + 128]
    if shift == 0:
        return first
    first = pltpu.roll(first, 128 - shift, 1)
    if 128 * block + 128 >= values.shape[1]:
        return first
    second = pltpu.roll(values[:, 128 * block + 128 : 128 * block + 256], 128 - shift, 1)
    return jnp.where(iota(first.shape, 1) < 128 - shift, first, second)


def send_all(peer_of, count, me, source, target, send_sem, recv_sem):
    for step in range(1, count):
        peer = (me + step) & (count - 1)
        pltpu.make_async_remote_copy(
            src_ref=source(peer),
            dst_ref=target(me),
            send_sem=send_sem,
            recv_sem=recv_sem,
            device_id=peer_of(peer),
            device_id_type=MESH,
        ).start()


def all_but_one(peer_of, count, me, target, send_sem, recv_sem):
    part = target(pl.ds(0, count - 1))
    return pltpu.make_async_remote_copy(
        src_ref=part,
        dst_ref=part,
        send_sem=send_sem,
        recv_sem=recv_sem,
        device_id=peer_of(lax.rem(me + 1, count)),
        device_id_type=MESH,
    )


def slot_sum(ref, count):
    total = ref[0].astype(F32)
    for slot in range(1, count):
        total = total + ref[slot].astype(F32)
    return total


def unit_backward(gradient, unit, length):
    return (gradient - unit * jnp.sum(unit * gradient, axis=1, keepdims=True)) / length


def kernel(
    scale_ref,
    bias_ref,
    probe_ref,
    text_ref,
    x_hbm,
    wkv_hbm,
    wout_hbm,
    wtext_hbm,
    order_hbm,
    sums_ref,
    gfeat_ref,
    x_ref,
    wk_ref,
    keys_ref,
    values_ref,
    sorted_ref,
    wv_ref,
    wout_ref,
    wout_t_ref,
    wtext_ref,
    order_ref,
    mask_ref,
    soft_ref,
    texts,
    images,
    slab_out,
    slab_in,
    feat_out,
    feat_in,
    iret_out,
    iret_half,
    iret_sum,
    iret_in,
    tret_out,
    tret_in,
    tgo_all,
    igo_all,
    small_out,
    small_in,
    last_out,
    last_in,
    tiny_out,
    tiny_in,
    part_ref,
    last_f32,
    heads_ref,
    load_sem,
    send_sem,
    recv_sem,
    share_sem,
    quarter_sem,
):
    l = lax.axis_index("loop")
    k = lax.axis_index("grp")
    c = (l & 1) * 4 + (k & 1) * 2 + ((l >> 1) & 1)
    s = (l & 12) + (k >> 1)

    def in_column(peer):
        return {
            "loop": (l & 12) + (peer & 1) * 2 + (peer >> 2),
            "grp": (k & 6) + ((peer >> 1) & 1),
        }

    def in_plane(peer):
        return {"loop": (peer & 12) + (l & 3), "grp": (peer & 3) * 2 + (k & 1)}

    barrier = pltpu.get_barrier_semaphore()
    for peer_of, count, me in ((in_plane, NP, s), (in_column, NC, c)):
        for step in range(1, count):
            pl.semaphore_signal(
                barrier,
                inc=1,
                device_id=peer_of((me + step) & (count - 1)),
                device_id_type=MESH,
            )

    def load(source, target, number):
        return pltpu.make_async_copy(source, target, load_sem.at[number])

    loads = [
        load(wtext_hbm, wtext_ref, 0),
        load(wkv_hbm.at[:, :D], wk_ref, 1),
        load(x_hbm, x_ref, 2),
        load(wkv_hbm.at[:, D:], wv_ref, 3),
        load(wout_hbm, wout_ref, 4),
        load(order_hbm, order_ref, 5),
    ]
    for number in range(3):
        loads[number].start()

    column = (in_column, NC, c)
    plane = (in_plane, NP, s)
    phases = {
        0: (plane, lambda i: texts.at[i]),
        1: (column, lambda i: images.at[i]),
        2: (plane, lambda i: tret_in.at[i]),
        4: (column, lambda i: slab_in.at[i]),
        5: (column, lambda i: igo_all.at[i]),
        6: (column, lambda i: tgo_all.at[i]),
        7: (column, lambda i: small_in.at[i]),
        8: (plane, lambda i: last_in.at[0, i]),
        9: (plane, lambda i: last_in.at[1, i]),
        10: (plane, lambda i: tiny_in.at[i]),
        11: (column, lambda i: feat_in.at[i]),
    }
    started = []

    def copies(phase):
        (peer_of, count, me), target = phases[phase]
        return all_but_one(peer_of, count, me, target, send_sem.at[phase], recv_sem.at[phase])

    def send(phase, source):
        (peer_of, count, me), target = phases[phase]
        send_all(peer_of, count, me, source, target, send_sem.at[phase], recv_sem.at[phase])
        started.append(phase)

    def block_copy(phase, slots, peer, number):
        block = phases[phase][1](slots)
        return pltpu.make_async_remote_copy(
            src_ref=block,
            dst_ref=block,
            send_sem=send_sem.at[phase],
            recv_sem=share_sem.at[phase, number],
            device_id=in_column(peer),
            device_id_type=MESH,
        )

    def share(phase):
        for step in (2, 1, 3):
            block_copy(phase, c, (c & 4) + ((c + step) & 3), step).start()
        block_copy(phase, c, c ^ 4, 0).start()
        started.append(phase)

    def arrive_shared(phase):
        for step in (1, 3, 2):
            slot = (c & 4) + ((c - step) & 3)
            block_copy(phase, slot, c ^ 4, step).wait_recv()
            block_copy(phase, slot, c ^ 4, 0).start()
        block_copy(phase, pl.ds((c & 4) ^ 4, 4), c ^ 4, 0).wait_recv()

    def arrive(phase):
        copies(phase).wait_recv()

    head_of_row = iota((HEADS * ROWS, D), 0) >> 4
    lane = iota((HEADS * ROWS, D), 1)
    in_head = (lane >= head_of_row * HEAD) & (lane < head_of_row * HEAD + HEAD)
    mask_ref[...] = jnp.where(in_head, 1.0, 0.0).astype(BF16)

    loads[0].wait()
    loads[3].start()
    text_out = nn(text_ref[...], wtext_ref[...])
    text_length = jnp.sqrt(jnp.sum(text_out * text_out, axis=1, keepdims=True) + 1e-06)
    text_unit = text_out / text_length
    texts[s] = text_unit.astype(BF16)

    query = probe_ref[...].reshape(1, D).astype(BF16).astype(F32)
    query_heads = (mask_ref[...].astype(F32) * query).astype(BF16)
    loads[1].wait()
    loads[2].wait()
    loads[4].start()
    loads[5].start()
    for block in range(3):
        columns = slice(384 * block, 384 * block + 384)
        keys_ref[:, columns] = nn(x_ref[...], wk_ref[:, columns]).astype(BF16)
        if block == 1:
            pl.semaphore_wait(barrier, NP + NC - 2)
            send(0, lambda p: texts.at[s])
    scores = nt(keys_ref[...], query_heads) / ROOT

    same = (iota((ROWS * PATCH, HEADS * ROWS), 0) >> 5) == (
        iota((ROWS * PATCH, HEADS * ROWS), 1) & (ROWS - 1)
    )
    highest = jnp.max(jnp.where(same, scores, -jnp.inf), axis=0, keepdims=True)
    powers = jnp.where(same, jnp.exp(scores - highest), 0.0)
    weights = powers / jnp.sum(powers, axis=0, keepdims=True)
    soft_ref[...] = weights
    weights_t = weights.T.astype(BF16)

    patch_sums = nn(weights_t, x_ref[...]).astype(BF16)
    loads[3].wait()
    mixed = nn(patch_sums, wv_ref[...]) * mask_ref[...].astype(F32)
    pooled = jnp.sum(mixed.reshape(HEADS, ROWS, D), axis=0)
    pooled_half = pooled.astype(BF16)
    loads[4].wait()
    image_out = nn(pooled_half, wout_ref[...])
    image_length = jnp.sqrt(jnp.sum(image_out * image_out, axis=1, keepdims=True) + 1e-06)
    image_unit = image_out / image_length
    images[c] = image_unit.astype(BF16)
    share(1)

    loads[5].wait()
    slab_out[...] = nt(order_ref[...], patch_sums).astype(BF16).reshape(NC, SLAB, HEADS * ROWS)
    slab_in[c] = slab_out[c]
    send(4, lambda p: slab_out.at[p])
    features = jnp.concatenate([pooled_half, text_ref[...]], axis=0)
    for place in range(NC):
        rows = order_ref[SLAB * place : SLAB * place + SLAB, :]
        feat_out[place, :, :SLAB] = nt(features, rows).astype(BF16)
    feat_in[c] = feat_out[c]
    send(11, lambda p: feat_out.at[p])

    for block in range(3):
        rows = slice(384 * block, 384 * block + 384)
        wout_t_ref[:, rows] = flip(wout_ref[rows, :])

    temperature = jnp.exp(scale_ref[...])
    arrive_shared(1)
    arrive(0)
    text_all = texts[...].reshape(NP * ROWS, D)
    image_all = images[...].reshape(NC * ROWS, D)
    logits = temperature * nt(image_all, text_all) + bias_ref[...]
    row = iota((NC * ROWS, NP * ROWS), 0)
    col = iota((NC * ROWS, NP * ROWS), 1)
    matched = ((row >> 4) == c) & ((col >> 4) == s) & ((row & 15) == (col & 15))
    sign = jnp.where(matched, 1.0, -1.0)
    coeff = -sign / (1.0 + jnp.exp(sign * logits))
    iret_out[...] = nn(coeff.astype(BF16), text_all).astype(BF16).reshape(NC, ROWS, D)
    halves = pltpu.make_async_remote_copy(
        src_ref=iret_out.at[pl.ds((c & 4) ^ 4, 4)],
        dst_ref=iret_half,
        send_sem=send_sem.at[3],
        recv_sem=recv_sem.at[3],
        device_id=in_column(c ^ 4),
        device_id_type=MESH,
    )
    halves.start()
    tret_out[...] = nn(flip(coeff), image_all).astype(BF16).reshape(NP, ROWS, D)
    tret_in[s] = tret_out[s]
    send(2, lambda p: tret_out.at[p])
    halves.wait_recv()
    iret_sum[...] = (
        iret_out[pl.ds(c & 4, 4)].astype(F32) + iret_half[...].astype(F32)
    ).astype(BF16)
    iret_in[c & 3] = iret_sum[c & 3]

    def quarter(step, slot):
        return pltpu.make_async_remote_copy(
            src_ref=iret_sum.at[slot],
            dst_ref=iret_in.at[c & 3],
            send_sem=quarter_sem.at[0, step],
            recv_sem=quarter_sem.at[1, step],
            device_id=in_column((c & 4) + slot),
            device_id_type=MESH,
        )

    quarters = [quarter(step, (c + step) & 3) for step in (2, 1, 3)]
    for copy in quarters:
        copy.start()

    for block in range(3):
        columns = slice(384 * block, 384 * block + 384)
        values_ref[:, columns] = nn(x_ref[...], wv_ref[:, columns]).astype(BF16)
        sorted_ref[:, columns] = nt(x_ref[...], order_ref[columns, :]).astype(BF16)
    last_f32[...] = jnp.zeros_like(last_f32)

    for copy in quarters:
        copy.wait_recv()
    image_returned = temperature * slot_sum(iret_in, 4)
    image_grad = unit_backward(image_returned, image_unit, image_length).astype(BF16)
    igo_all[c] = image_grad
    share(5)

    pooled_grad = nn(image_grad, wout_t_ref[...]).astype(BF16).astype(F32)
    tiled = jnp.concatenate([pooled_grad] * HEADS, axis=0)
    grad_heads = (mask_ref[...].astype(F32) * tiled).astype(BF16)
    weight_grad = nt(values_ref[...], grad_heads)
    weights = soft_ref[...]
    inner = jnp.sum(weights * weight_grad, axis=0, keepdims=True)
    score_grad = (weights * (weight_grad - inner)).astype(BF16)
    fold = jnp.where((iota((HEADS * ROWS, 128), 0) >> 4) == iota((HEADS * ROWS, 128), 1), 1.0, 0.0)
    score_grad_t = nn(score_grad, fold.astype(BF16)).T[:HEADS].astype(BF16)

    arrive(2)
    text_returned = temperature * slot_sum(tret_in, NP)
    text_grad = unit_backward(text_returned, text_unit, text_length).astype(BF16)
    tgo_all[c] = text_grad
    share(6)

    key_sum = nn(score_grad_t, sorted_ref[...])
    head_row = iota((HEADS, D), 0)
    head_col = iota((HEADS, D), 1)
    own_head = (head_col >= head_row * HEAD) & (head_col < head_row * HEAD + HEAD)
    probe_sum = jnp.where(own_head, nn(score_grad_t, keys_ref[...]), 0.0) / ROOT
    tile_row = iota((HEADS, 128), 0)
    tile_lane = iota((HEADS, 128), 1)
    probe_tile = jnp.zeros((HEADS, 128), F32)
    for head in range(HEADS):
        probe_tile = jnp.where(tile_row == head, slab_of(probe_sum, HEAD * head), probe_tile)
    probe_tile = pltpu.roll(probe_tile, SPARE, 1)
    for place in range(NC):
        start = SLAB * place
        small_out[place, :, :128] = slab_of(key_sum, start)
        small_out[place, :, 128:] = jnp.where(
            tile_lane < SPARE, slab_of(key_sum, start + 128), probe_tile
        )
    small_in[c] = small_out[c]
    send(7, lambda p: small_out.at[p])


    def place_rows(offset):
        for part in range(NP):
            last_f32[32 * part + offset : 32 * part + offset + OWN, :] = part_ref[
                OWN * part : OWN * part + OWN, :
            ]

    arrive(11)
    arrive_shared(5)
    igo = igo_all[...].reshape(NC * ROWS, D)
    part_ref[...] = nn(flip(feat_in[:, :ROWS, :].reshape(NC * ROWS, 256))[:SLAB], igo)
    place_rows(0)
    pooled_grads = nn(igo, wout_t_ref[...]).astype(BF16)
    for place in range(NC):
        tiled = jnp.concatenate([pooled_grads[ROWS * place : ROWS * place + ROWS]] * HEADS, axis=0)
        heads_ref[256 * place : 256 * place + 256, :] = mask_ref[...] * tiled
    arrive(4)
    left = jnp.concatenate([slab_in[place] for place in range(NC)], axis=1)
    part_ref[...] = nn(left, heads_ref[...])
    place_rows(OWN)

    def pack(half):
        rows = last_f32[...].reshape(NP, 32, D)[:, 16 * half : 16 * half + 16]
        last_out[half] = rows.astype(BF16)
        last_in[half, s] = last_out[half, s]

    pack(0)
    send(8, lambda p: last_out.at[0, p])

    arrive_shared(6)
    tgo = tgo_all[...].reshape(NC * ROWS, D)
    part_ref[...] = nn(flip(feat_in[:, ROWS:, :].reshape(NC * ROWS, 256))[:SLAB], tgo)
    place_rows(2 * OWN)
    pack(1)
    arrive(7)
    tiny = slot_sum(small_in, NC)
    for place in range(NP):
        tiny_out[place] = jnp.where(
            tile_lane < SPARE, slab_of(tiny, OWN * place), tiny[:, 128:]
        )
    tiny_in[s] = tiny_out[s]
    send(10, lambda p: tiny_out.at[p])

    send(9, lambda p: last_out.at[1, p])

    gfeat_ref[...] = nt(text_grad, wtext_ref[...]).astype(BF16)

    arrive(10)
    tiny = slot_sum(tiny_in, NP)
    probe_tile = pltpu.roll(tiny, 128 - SPARE, 1)
    spread = jnp.where(iota((128, D), 0) == iota((1, D), 1) % HEAD, 1.0, 0.0)
    probe_grad = exact(probe_tile, spread)
    sums_ref[48:56, :] = jnp.broadcast_to(
        jnp.sum(jnp.where(own_head, probe_grad, 0.0), axis=0, keepdims=True), (8, D)
    )
    sums_ref[32:48, :] = exact(tiny.T[:16, :], jnp.where(own_head, query, 0.0) / ROOT)

    arrive(8)
    sums_ref[:16, :] = slot_sum(last_in.at[0], NP)
    arrive(9)
    sums_ref[16:32, :] = slot_sum(last_in.at[1], NP)

    for copy in [halves] + quarters:
        copy.wait_send()
    for phase in started:
        copies(phase).wait_send()


def part_sums(sums_ref, feat_ref, gkv_ref, gout_ref, gtext_ref, gprobe_ref, gfeat_ref):
    gout_ref[...] = sums_ref[:OWN, :]
    gkv_ref[:, :D] = sums_ref[32 : 32 + OWN, :]
    gkv_ref[:, D:] = sums_ref[OWN : 2 * OWN, :]
    gtext_ref[...] = sums_ref[2 * OWN : 3 * OWN, :]
    gprobe_ref[...] = sums_ref[48:49, :].reshape(D)
    gfeat_ref[...] = feat_ref[...]


def column_order():
    c, s, r = np.meshgrid(np.arange(NC), np.arange(NP), np.arange(OWN), indexing="ij")
    loop = (s // 4) * 4 + (c % 2) * 2 + c // 4
    grp = (s % 4) * 2 + c // 2 % 2
    kept = ((loop * 8 + grp) * OWN + r).reshape(D)
    return (kept[:, None] == np.arange(D)[None, :]).astype(ml_dtypes.bfloat16)


def shards(patches, probe, key_value_matrix, output_weight, text, text_weight, log_scale, bias):
    vmem = pl.BlockSpec(memory_space=pltpu.VMEM)
    anywhere = pl.BlockSpec(memory_space=pl.ANY)
    sums = pl.pallas_call(
        kernel,
        out_shape=(
            jax.ShapeDtypeStruct((56, D), F32),
            jax.ShapeDtypeStruct((ROWS, D), BF16),
        ),
        in_specs=[vmem] * 4 + [anywhere] * 5,
        out_specs=(vmem,) * 2,
        scratch_shapes=[
            pltpu.VMEM((ROWS * PATCH, D), BF16),
            pltpu.VMEM((D, D), BF16),
            pltpu.VMEM((ROWS * PATCH, D), BF16),
            pltpu.VMEM((ROWS * PATCH, D), BF16),
            pltpu.VMEM((ROWS * PATCH, D), BF16),
            pltpu.VMEM((D, D), BF16),
            pltpu.VMEM((D, D), BF16),
            pltpu.VMEM((D, D), BF16),
            pltpu.VMEM((D, D), BF16),
            pltpu.VMEM((D, D), BF16),
            pltpu.VMEM((HEADS * ROWS, D), BF16),
            pltpu.VMEM((ROWS * PATCH, HEADS * ROWS), F32),
            pltpu.VMEM((NP, ROWS, D), BF16),
            pltpu.VMEM((NC, ROWS, D), BF16),
            pltpu.VMEM((NC, SLAB, HEADS * ROWS), BF16),
            pltpu.VMEM((NC, SLAB, HEADS * ROWS), BF16),
            pltpu.VMEM((NC, 2 * ROWS, HEADS * ROWS), BF16),
            pltpu.VMEM((NC, 2 * ROWS, HEADS * ROWS), BF16),
            pltpu.VMEM((NC, ROWS, D), BF16),
            pltpu.VMEM((4, ROWS, D), BF16),
            pltpu.VMEM((4, ROWS, D), BF16),
            pltpu.VMEM((4, ROWS, D), BF16),
            pltpu.VMEM((NP, ROWS, D), BF16),
            pltpu.VMEM((NP, ROWS, D), BF16),
            pltpu.VMEM((NC, ROWS, D), BF16),
            pltpu.VMEM((NC, ROWS, D), BF16),
            pltpu.VMEM((NC, HEADS, 256), F32),
            pltpu.VMEM((NC, HEADS, 256), F32),
            pltpu.VMEM((2, NP, 16, D), BF16),
            pltpu.VMEM((2, NP, 16, D), BF16),
            pltpu.VMEM((NP, HEADS, 128), F32),
            pltpu.VMEM((NP, HEADS, 128), F32),
            pltpu.VMEM((SLAB, D), F32),
            pltpu.VMEM((NP * 32, D), F32),
            pltpu.VMEM((NC * HEADS * ROWS, D), BF16),
            pltpu.SemaphoreType.DMA((6,)),
            pltpu.SemaphoreType.DMA((12,)),
            pltpu.SemaphoreType.DMA((12,)),
            pltpu.SemaphoreType.DMA((11, 4)),
            pltpu.SemaphoreType.DMA((2, 4)),
        ],
        compiler_params=pltpu.CompilerParams(
            collective_id=0, has_side_effects=True, vmem_limit_bytes=56 * 1024 * 1024
        ),
    )(
        log_scale.reshape(1, 1),
        bias.reshape(1, 1),
        probe,
        text,
        patches.reshape(ROWS * PATCH, D),
        key_value_matrix,
        output_weight,
        text_weight,
        jnp.asarray(column_order()),
    )
    return pl.pallas_call(
        part_sums,
        out_shape=(
            jax.ShapeDtypeStruct((OWN, 2 * D), F32),
            jax.ShapeDtypeStruct((OWN, D), F32),
            jax.ShapeDtypeStruct((OWN, D), F32),
            jax.ShapeDtypeStruct((D,), F32),
            jax.ShapeDtypeStruct((ROWS, D), BF16),
        ),
        in_specs=[vmem] * 2,
        out_specs=(vmem,) * 5,
    )(*sums)


def solution(mesh):
    rows = P(("loop", "grp"), None)
    return jax.shard_map(
        shards,
        mesh=mesh,
        in_specs=(P(("loop", "grp"), None, None), P(), P(), P(), rows, P(), P(), P()),
        out_specs=(rows, rows, rows, P(), rows),
        check_vma=False,
    )
```
